512 devices in a mesh: dp: 4 (over z_lo), view: 8 (over x, core), frame: 16 (over z_hi, y).
Axes of the slice: x: 4, y: 8, z: 8 (z_hi: 2, z_lo: 4; z = z_hi * 4 + z_lo), core: 2. Of those that a mesh axis runs over, the one named last changes fastest.
Arguments:
- query_rows: bfloat16 [4, 8, 16, 128, 1024], P('dp', 'view', 'frame'), may hold values from -8 to 8
- key_rows: bfloat16 [4, 8, 16, 128, 1024], P('dp', 'view', 'frame'), may hold values from -8 to 8
- value_rows: bfloat16 [4, 8, 16, 128, 1024], P('dp', 'view', 'frame'), may hold values from -6 to 6
- cotangent: bfloat16 [4, 8, 16, 128, 1024], P('dp', 'view', 'frame'), may hold values from -6 to 6
- out_weight: bfloat16 [1024, 1024], P('frame'), may hold values from -0.1875 to 0.1875
Outputs:
- projected: bfloat16 [4, 8, 16, 128, 1024], P('dp', 'view', 'frame')
- query_grad: bfloat16 [4, 8, 16, 128, 1024], P('dp', 'view', 'frame')
- key_grad: bfloat16 [4, 8, 16, 128, 1024], P('dp', 'view', 'frame')
- value_grad: bfloat16 [4, 8, 16, 128, 1024], P('dp', 'view', 'frame')
- weight_grad: bfloat16 [1024, 1024], P(('view', 'frame'))
The draws below stay inside these ranges and needn't reach their ends.
All inputs are finite; a program needn't handle non-finite values.
Results may differ from the reference program's by a relative error of at most 0.012.
Values may be sent and summed in bfloat16 or wider, within the bound.
A program may use at most 128 MiB of HBM per device.

```python
import jax
import jax.numpy as jnp
from jax import lax

D = 1024
HEADS = 16
HEAD_DIM = 64
POS = 128
SAMPLES = 4
VIEWS = 8
FRAMES = 16
TOKENS = 65536


def draw_query_rows(key, part):
    key = jax.random.fold_in(key, 1)
    full_shape = (SAMPLES, VIEWS, FRAMES, POS, D)
    return jnp.clip(jax.random.normal(key, full_shape), -6.0, 6.0).astype(jnp.bfloat16)


def draw_key_rows(key, part):
    key = jax.random.fold_in(key, 2)
    full_shape = (SAMPLES, VIEWS, FRAMES, POS, D)
    return jnp.clip(jax.random.normal(key, full_shape), -6.0, 6.0).astype(jnp.bfloat16)


def block_scale(own_key, dims, cuts, least, largest):
    gain = 1.0
    for dim, parts in cuts:
        draws = jax.random.uniform(jax.random.fold_in(jax.random.fold_in(own_key, 6), dim), (parts,), jnp.float32, least / len(cuts), largest / len(cuts))
        gain = gain * jnp.repeat(jnp.exp(draws), dims[dim] // parts).reshape((-1,) + (1,) * (len(dims) - 1 - dim))
    return gain


def gaussian(key, extent, width, most, shards=(), kind=jnp.bfloat16):
    entries = jax.random.normal(key, extent, jnp.float32) * width
    if len(shards) > 0:
        entries = block_scale(key, extent, shards, -0.22, 0.18) * entries
    return jnp.clip(entries, min=-most, max=most).astype(kind)


def setup_inputs(seed: int = 0) -> dict:
    keys = jax.random.split(jax.random.key(seed), 6)
    return {
        "query_rows": draw_query_rows(jax.random.fold_in(keys[5], 71), 0),
        "key_rows": draw_key_rows(jax.random.fold_in(keys[5], 71), 0),
        "value_rows": gaussian(keys[2], (SAMPLES, VIEWS, FRAMES, POS, D), 1.0, 6.0, ((0, 4), (1, 8), (2, 16))),
        "cotangent": gaussian(keys[3], (SAMPLES, VIEWS, FRAMES, POS, D), 1.0, 6.0, ((0, 4), (1, 8), (2, 16))),
        "out_weight": gaussian(keys[4], (D, D), D ** -0.5, 0.1875, ((0, 16),)),
    }


def softmax_rows(scores):
    highest = jnp.max(scores, axis=-1, keepdims=True)
    raised = jnp.exp(scores - highest)
    return raised / jnp.sum(raised, axis=-1, keepdims=True)


def score_block(head_queries, head_keys):
    products = jnp.einsum("blhd,bmhd->bhlm", head_queries.astype(jnp.float32), head_keys.astype(jnp.float32))
    return products * (HEAD_DIM ** -0.5)


def attend_forward(head_queries, head_keys, head_values):
    probabilities = softmax_rows(score_block(head_queries, head_keys))
    weights = lax.optimization_barrier(probabilities.astype(jnp.bfloat16)).astype(jnp.float32)
    mixed_heads = jnp.einsum("bhlm,bmhd->blhd", weights, head_values.astype(jnp.float32))
    return mixed_heads.astype(jnp.bfloat16)


def attend_backward(head_queries, head_keys, head_values, grad_block):
    probabilities = softmax_rows(score_block(head_queries, head_keys))
    weights = lax.optimization_barrier(probabilities.astype(jnp.bfloat16)).astype(jnp.float32)
    grad_float = grad_block.astype(jnp.float32)
    value_part = jnp.einsum("bhlm,blhd->bmhd", weights, grad_float).astype(jnp.bfloat16)
    dprob = jnp.einsum("blhd,bmhd->bhlm", grad_float, head_values.astype(jnp.float32))
    row_delta = jnp.sum(probabilities * dprob, axis=-1, keepdims=True)
    dscore = lax.optimization_barrier((probabilities * (dprob - row_delta)).astype(jnp.bfloat16)).astype(jnp.float32)
    query_part = (jnp.einsum("bhlm,bmhd->blhd", dscore, head_keys.astype(jnp.float32)) * (HEAD_DIM ** -0.5)).astype(jnp.bfloat16)
    key_part = (jnp.einsum("bhlm,blhd->bmhd", dscore, head_queries.astype(jnp.float32)) * (HEAD_DIM ** -0.5)).astype(jnp.bfloat16)
    return query_part, key_part, value_part


def to_heads(sample_block, length_axis):
    moved_block = jnp.moveaxis(sample_block, length_axis, 2)
    heads = moved_block.reshape((-1, moved_block.shape[2], HEADS, HEAD_DIM))
    return heads, moved_block.shape


def from_heads(heads, moved_shape, length_axis):
    return jnp.moveaxis(heads.reshape(moved_shape), 2, length_axis)


def batched(function, arrays, pieces):
    split_arrays = tuple(array_part.reshape((pieces, array_part.shape[0] // pieces) + array_part.shape[1:]) for array_part in arrays)
    result = lax.map(lambda grouped: function(*grouped), split_arrays)
    return jax.tree.map(lambda leaf_array: leaf_array.reshape((-1,) + leaf_array.shape[2:]), result)


def piece_count(heads, length_axis):
    if length_axis == 2:
        return max(1, heads.shape[0] // 16)
    return 1


def sample_forward(sample_queries, sample_keys, sample_values):
    running_total = jnp.zeros(sample_queries.shape, jnp.float32)
    for length_axis in (2, 0, 1):
        head_queries, moved_shape = to_heads(sample_queries, length_axis)
        head_keys, moved_shape = to_heads(sample_keys, length_axis)
        head_values, moved_shape = to_heads(sample_values, length_axis)
        pieces = piece_count(head_queries, length_axis)
        mixed_heads = batched(attend_forward, (head_queries, head_keys, head_values), pieces)
        running_total = running_total + from_heads(mixed_heads, moved_shape, length_axis).astype(jnp.float32)
    return running_total.astype(jnp.bfloat16)


def sample_backward(sample_queries, sample_keys, sample_values, sample_grad):
    totals = [jnp.zeros(sample_queries.shape, jnp.float32) for index_name in range(3)]
    for length_axis in (2, 0, 1):
        head_queries, moved_shape = to_heads(sample_queries, length_axis)
        head_keys, moved_shape = to_heads(sample_keys, length_axis)
        head_values, moved_shape = to_heads(sample_values, length_axis)
        head_grad, moved_shape = to_heads(sample_grad, length_axis)
        pieces = piece_count(head_queries, length_axis)
        terms = batched(attend_backward, (head_queries, head_keys, head_values, head_grad), pieces)
        totals = [running + from_heads(term_part, moved_shape, length_axis).astype(jnp.float32) for running, term_part in zip(totals, terms)]
    return tuple(running.astype(jnp.bfloat16) for running in totals)


def reference(query_rows, key_rows, value_rows, cotangent, out_weight):
    attended = lax.map(lambda grouped: sample_forward(*grouped), (query_rows, key_rows, value_rows))
    flat_attended = attended.reshape((-1, D))
    flat_grad = cotangent.reshape((-1, D))
    projected = jnp.dot(flat_attended, out_weight, preferred_element_type=jnp.float32).astype(jnp.bfloat16).reshape(query_rows.shape)
    grad_attended = jnp.dot(flat_grad, out_weight.T, preferred_element_type=jnp.float32).astype(jnp.bfloat16).reshape(query_rows.shape)
    grad_attended = lax.optimization_barrier(grad_attended)
    weight_grad = (jnp.dot(flat_attended.T, flat_grad, preferred_element_type=jnp.float32) * (TOKENS ** -0.5)).astype(jnp.bfloat16)
    query_grad, key_grad, value_grad = lax.map(lambda grouped: sample_backward(*grouped), (query_rows, key_rows, value_rows, grad_attended))
    return (projected, query_grad, key_grad, value_grad, weight_grad)
```

```python
import functools

import jax
import jax.numpy as jnp
from jax import lax
from jax.experimental import pallas as pl
from jax.experimental.pallas import tpu as pltpu
from jax.sharding import PartitionSpec as P

F32 = jnp.float32
BF16 = jnp.bfloat16
MESH = pl.DeviceIdType.MESH
NN = (((1,), (0,)), ((), ()))
NT = (((1,), (1,)), ((), ()))
TN = (((0,), (0,)), ((), ()))
MASKED = -1e30

D = 1024
VIEWS = 8
FRAMES = 16
CHIPS = VIEWS // 2
PAIRS = D // 128
HALF = D // 2
SCALE = 0.125


def dot(left, right, dims):
    return lax.dot_general(left, right, dims, preferred_element_type=F32)


def flat(block):
    return block.reshape(block.shape[0] * block.shape[1], block.shape[2])


def blocks(rows):
    return rows.reshape(rows.shape[0] // 8, 8, rows.shape[1])


def lower_lanes():
    return lax.broadcasted_iota(jnp.int32, (128, 128), 1) < 64


def by_head(rows, lower):
    one = lower.astype(F32).astype(BF16)
    other = (1.0 - lower.astype(F32)).astype(BF16)
    return jnp.concatenate([rows * one, rows * other], axis=0)


def group_bias(modulus):
    row = lax.broadcasted_iota(jnp.int32, (128, 128), 0)
    column = lax.broadcasted_iota(jnp.int32, (128, 128), 1)
    same = lax.rem(row, modulus) == lax.rem(column, modulus)
    return jnp.where(same, 0.0, MASKED).astype(F32)


def forward_pair(query, key, value, bias, lower):
    scores = dot(by_head(key, lower), query, NT) * SCALE
    halves = []
    for head in range(2):
        part = scores[128 * head : 128 * head + 128]
        if bias is not None:
            part = part + bias
        raised = jnp.exp(part - jnp.max(part, axis=0, keepdims=True))
        halves.append(raised * (1.0 / jnp.sum(raised, axis=0, keepdims=True)))
    probs = jnp.concatenate(halves, axis=0)
    out = dot(probs.astype(BF16), by_head(value, lower), TN)
    return probs, out


def backward_pair(query, key, value, grad, probs, lower):
    dprob = dot(by_head(value, lower), grad, NT)
    halves = []
    for head in range(2):
        prob = probs[128 * head : 128 * head + 128]
        term = prob * dprob[128 * head : 128 * head + 128]
        halves.append((term - prob * jnp.sum(term, axis=0, keepdims=True)).astype(BF16))
    dscore = jnp.concatenate(halves, axis=0)
    value_grad = dot(probs.astype(BF16), grad, NN)
    value_grad = jnp.where(lower, value_grad[:128], value_grad[128:])
    key_grad = dot(dscore, query, NN)
    key_grad = jnp.where(lower, key_grad[:128], key_grad[128:]) * SCALE
    query_grad = dot(dscore, by_head(key, lower), TN) * SCALE
    return query_grad, key_grad, value_grad


def frame_offset(step):
    far = lax.rem(step, 2)
    turn = step // 2
    odd = lax.rem(turn, 2)
    near = odd * ((turn + 1) // 2) + (1 - odd) * lax.rem(8 - turn // 2, 8)
    return near, far


def kernel(
    q_hbm, k_hbm, v_hbm, c_hbm, w_hbm,
    proj_hbm, dq_hbm, dk_hbm, dv_hbm, wg_hbm,
    own, of_view, of_frame, shard, weight,
    own_res, view_res, frame_res, view_back, frame_back,
    own_probs, view_probs, grad, rows,
    core_out, core_in, chip_out, chip_in, frame_out, frame_in, sample_out, sample_in,
    results, last,
    load_sem, store_sem, send_sem, recv_sem, core_send, core_recv, chip_send, chip_recv,
    slice_send, slice_recv, pass_send, pass_recv,
):
    sample = lax.axis_index("dp")
    view = lax.axis_index("view")
    frame = lax.axis_index("frame")
    chip = view // 2
    core = lax.rem(view, 2)
    far = frame // 8
    near = lax.rem(frame, 8)
    partner = {"view": chip * 2 + 1 - core}

    def frame_peer(step):
        by, across = frame_offset(step)
        return lax.rem(far + across, 2) * 8 + lax.rem(near + by, 8)

    def view_peer(step):
        return lax.rem(view + step, VIEWS)

    def sample_peer(step):
        return lax.rem(sample + step, 4)

    def chip_peer(step):
        return lax.rem(chip + step, CHIPS)

    def chip_device(step):
        return {"view": chip_peer(step) * 2 + core}

    def remote(source, target, send, recv, device):
        return pltpu.make_async_remote_copy(
            src_ref=source, dst_ref=target, send_sem=send, recv_sem=recv,
            device_id=device, device_id_type=MESH,
        )

    def each(first, last_step, body):
        def step(index, carry):
            body(index)
            return carry

        lax.fori_loop(first, last_step, step, 0)

    loads = [pltpu.make_async_copy(w_hbm, shard, load_sem.at[4])]
    for index, source in enumerate((q_hbm, k_hbm, v_hbm, c_hbm)):
        loads.append(pltpu.make_async_copy(source, own.at[index], load_sem.at[index]))
    for load in loads:
        load.start()
    barrier = pltpu.get_barrier_semaphore()

    def greet(device):
        pl.semaphore_signal(barrier, inc=1, device_id=device, device_id_type=MESH)

    each(1, FRAMES, lambda step: greet({"frame": frame_peer(step)}))
    each(1, VIEWS, lambda step: greet({"view": view_peer(step)}))
    each(1, 4, lambda step: greet({"dp": sample_peer(step)}))
    pl.semaphore_wait(barrier, FRAMES - 1 + VIEWS - 1 + 3)

    columns = pl.ds(pl.multiple_of(view * 128, 128), 128)
    shard_rows = pl.ds(pl.multiple_of(frame * 64, 64), 64)
    loads[0].wait()

    def send_weight(step):
        remote(
            shard.at[:, columns], weight.at[shard_rows, columns], send_sem.at[0], recv_sem.at[0],
            {"frame": frame_peer(step)},
        ).start()

    each(1, FRAMES, send_weight)
    for load in loads[1:]:
        load.wait()

    def send_view(step):
        peer = view_peer(step)
        remote(
            own.at[:, pl.ds(peer * 2, 2)], of_view.at[:, pl.ds(view * 2, 2)], send_sem.at[1], recv_sem.at[1],
            {"view": peer},
        ).start()

    def send_frame_grad(step):
        peer = frame_peer(step)
        remote(own.at[3, peer], of_frame.at[3, frame], send_sem.at[2], recv_sem.at[2], {"frame": peer}).start()

    def send_frame_rows(half):
        lanes = pl.ds(half * HALF, HALF)

        def send(step):
            peer = frame_peer(step)
            remote(
                own.at[pl.ds(0, 3), peer, :, lanes], of_frame.at[pl.ds(0, 3), frame, :, lanes],
                send_sem.at[3 + half], recv_sem.at[3 + half], {"frame": peer},
            ).start()

        return send

    each(1, VIEWS, send_view)
    each(1, FRAMES, send_frame_grad)
    each(1, FRAMES, send_frame_rows(0))
    each(1, FRAMES, send_frame_rows(1))

    weight[shard_rows, columns] = shard[:, columns]
    of_frame[:, pl.ds(frame, 1)] = own[:, pl.ds(frame, 1)]
    of_view[:, pl.ds(view * 2, 2)] = own[:, pl.ds(view * 2, 2)]

    lower = lower_lanes()

    def lanes_of(pair):
        return pl.ds(pl.multiple_of(pair * 128, 128), 128)

    def forward(source, target, kept, bias):
        def step(pair):
            lanes = lanes_of(pair)
            query, key, value = (flat(source[index, :, :, lanes]) for index in range(3))
            probs, out = forward_pair(query, key, value, bias, lower)
            kept[pair] = probs
            target[0, :, :, lanes] = blocks(out.astype(BF16))

        def two(index):
            step(index * 2)
            step(index * 2 + 1)

        each(0, PAIRS // 2, two)

    def grad_rows(source):
        cotangent = flat(source[3])
        for part in range(4):
            wide = slice(256 * part, 256 * part + 256)
            grad[:, wide] = dot(cotangent, weight[wide, :], NT).astype(BF16)

    def backward_step(source, target, probs, pair):
        lanes = lanes_of(pair)
        query, key, value = (flat(source[index, :, :, lanes]) for index in range(3))
        grads = backward_pair(query, key, value, grad[:, lanes], probs, lower)
        for index, term in enumerate(grads):
            target[1 + index, :, :, lanes] = blocks(term.astype(BF16))

    def backward(source, target, kept):
        grad_rows(source)

        def two(index):
            for pair in (index * 2, index * 2 + 1):
                backward_step(source, target, kept[pair], pair)

        each(0, PAIRS // 2, two)

    forward(own, own_res, own_probs, None)

    gathered = remote(
        weight.at[pl.ds(0, 64 * (FRAMES - 1)), columns], weight.at[pl.ds(0, 64 * (FRAMES - 1)), columns],
        send_sem.at[0], recv_sem.at[0], partner,
    )
    gathered.wait_recv()
    slices = []
    for step in (1, 3, 2):
        slices.append(
            remote(
                weight.at[:, columns], weight.at[:, columns], slice_send.at[step], slice_recv.at[step],
                chip_device(step),
            )
        )
    passes = [remote(weight.at[:, columns], weight.at[:, columns], pass_send.at[0], pass_recv.at[0], partner)]
    for copy in slices + passes:
        copy.start()

    view_bytes = remote(
        own.at[:, pl.ds(0, 2 * (VIEWS - 1))], of_view.at[:, pl.ds(0, 2 * (VIEWS - 1))], send_sem.at[1],
        recv_sem.at[1], partner,
    )
    view_bytes.wait_recv()
    forward(of_view, view_res, view_probs, group_bias(16))

    for copy, step in zip(slices, (1, 3, 2)):
        copy.wait_recv()
        came = lax.rem(chip + CHIPS - step, CHIPS) * 2 + core
        there = pl.ds(pl.multiple_of(came * 128, 128), 128)
        onward = remote(weight.at[:, there], weight.at[:, there], pass_send.at[step], pass_recv.at[step], partner)
        onward.start()
        passes.append(onward)
    for onward in passes:
        onward.wait_recv()

    backward(of_view, view_res, view_probs)

    def return_view(step):
        peer = view_peer(step)
        remote(
            view_res.at[:, pl.ds(peer * 2, 2)], view_back.at[:, pl.ds(view * 2, 2)], send_sem.at[5], recv_sem.at[5],
            {"view": peer},
        ).start()

    each(1, VIEWS, return_view)
    view_back[:, pl.ds(view * 2, 2)] = view_res[:, pl.ds(view * 2, 2)]

    others = FRAMES - 1
    remote(
        own.at[3, pl.ds(0, others)], of_frame.at[3, pl.ds(0, others)], send_sem.at[2], recv_sem.at[2], partner
    ).wait_recv()
    grad_rows(of_frame)
    frame_bias = group_bias(8)

    def rows_of_half(half, source, target, slot):
        lanes = pl.ds(half * HALF, HALF)
        parts = pl.ds(0, 3) if slot < 5 else pl.ds(0, 4)
        return remote(
            source.at[parts, pl.ds(0, others), :, lanes], target.at[parts, pl.ds(0, others), :, lanes],
            send_sem.at[slot], recv_sem.at[slot], partner,
        )

    def return_frame(half):
        lanes = pl.ds(half * HALF, HALF)

        def send(step):
            peer = frame_peer(step)
            remote(
                frame_res.at[:, peer, :, lanes], frame_back.at[:, frame, :, lanes],
                send_sem.at[6 + half], recv_sem.at[6 + half], {"frame": peer},
            ).start()

        return send

    def frame_step(pair):
        lanes = lanes_of(pair)
        query, key, value = (flat(of_frame[index, :, :, lanes]) for index in range(3))
        probs, out = forward_pair(query, key, value, frame_bias, lower)
        frame_res[0, :, :, lanes] = blocks(out.astype(BF16))
        backward_step(of_frame, frame_res, probs, pair)

    for half in range(2):
        rows_of_half(half, own, of_frame, 3 + half).wait_recv()

        def two(index):
            frame_step(half * (PAIRS // 2) + index * 2)
            frame_step(half * (PAIRS // 2) + index * 2 + 1)

        each(0, PAIRS // 4, two)
        each(1, FRAMES, return_frame(half))
        wide = slice(half * HALF, half * HALF + HALF)
        frame_back[:, pl.ds(frame, 1), :, wide] = frame_res[:, pl.ds(frame, 1), :, wide]

    for index, source in enumerate((own, of_view, of_frame)):
        rows[128 * index : 128 * index + 128] = flat(source[3])

    def gradient_rows(which):
        lanes = lanes_of(which)
        left = jnp.concatenate(
            [flat(res[0, :, :, lanes]) for res in (own_res, view_res, frame_res)], axis=0
        )
        return [dot(left, rows[:, HALF * part : HALF * part + HALF], TN) for part in range(2)]

    to_core = []
    for slot, step in enumerate((1, 3, 2, 0)):
        for part, value in enumerate(gradient_rows(chip_peer(step) * 2 + 1 - core)):
            core_out[slot, :, :, HALF * part : HALF * part + HALF] = blocks(value.astype(BF16))
        copy = remote(core_out.at[slot], core_in.at[slot], core_send.at[slot], core_recv.at[slot], partner)
        copy.start()
        to_core.append(copy)
    to_chip = []
    for slot, step in enumerate((1, 3, 2, 0)):
        values = gradient_rows(chip_peer(step) * 2 + core)
        to_core[slot].wait_recv()
        for part, value in enumerate(values):
            wide = slice(HALF * part, HALF * part + HALF)
            chip_out[slot, :, :, wide] = blocks((value + flat(core_in[slot, :, :, wide]).astype(F32)).astype(BF16))
        if step > 0:
            copy = remote(
                chip_out.at[slot], chip_in.at[slot], chip_send.at[slot], chip_recv.at[slot], chip_device(step)
            )
            copy.start()
            to_chip.append(copy)

    backward(own, own_res, own_probs)

    for copy in to_chip:
        copy.wait_recv()
    for part in range(4):
        wide = slice(256 * part, 256 * part + 256)
        total = chip_out[3, :, :, wide].astype(F32)
        for slot in range(3):
            total = total + chip_in[slot, :, :, wide].astype(F32)
        frame_out[:, :, wide] = total.astype(BF16)

    def send_gradient(step):
        peer = frame_peer(step)
        remote(frame_out.at[peer], frame_in.at[frame], send_sem.at[8], recv_sem.at[8], {"frame": peer}).start()

    each(1, FRAMES, send_gradient)
    frame_in[pl.ds(frame, 1)] = frame_out[pl.ds(frame, 1)]

    remote(
        view_res.at[:, pl.ds(0, 2 * (VIEWS - 1))], view_back.at[:, pl.ds(0, 2 * (VIEWS - 1))], send_sem.at[5],
        recv_sem.at[5], partner,
    ).wait_recv()
    for half in range(2):
        rows_of_half(half, frame_res, frame_back, 6 + half).wait_recv()
        for index in range(4):
            for part in range(2):
                wide = slice(half * HALF + 256 * part, half * HALF + 256 * part + 256)
                total = own_res[index, :, :, wide].astype(F32) + view_back[index, :, :, wide].astype(F32)
                total = total + frame_back[index, :, :, wide].astype(F32)
                results[index, :, :, wide] = total.astype(BF16)
    stores = []
    for index, target in ((1, dq_hbm), (2, dk_hbm), (3, dv_hbm)):
        stores.append(pltpu.make_async_copy(results.at[index], target, store_sem.at[index]))
    for store in stores:
        store.start()
    attended = flat(results[0])
    for part in range(4):
        wide = slice(256 * part, 256 * part + 256)
        own_res[0, :, :, wide] = blocks(dot(attended, weight[:, wide], NN).astype(BF16))
    stores.append(pltpu.make_async_copy(own_res.at[0], proj_hbm, store_sem.at[0]))
    stores[-1].start()

    remote(
        frame_out.at[pl.ds(0, others)], frame_in.at[pl.ds(0, others)], send_sem.at[8], recv_sem.at[8], partner
    ).wait_recv()
    total = frame_in[0].astype(F32)
    for index in range(1, FRAMES):
        total = total + frame_in[index].astype(F32)
    sample_out[...] = total
    to_sample = []
    for step in (1, 2, 3):
        copy = remote(
            sample_out, sample_in.at[step], core_send.at[3 + step], core_recv.at[3 + step], {"dp": sample_peer(step)}
        )
        copy.start()
        to_sample.append(copy)
    for copy in to_sample:
        copy.wait_recv()
    total = sample_out[...]
    for step in (1, 2, 3):
        total = total + sample_in[step]
    last[...] = (total * (1.0 / 256.0)).astype(BF16)
    stores.append(pltpu.make_async_copy(last, wg_hbm, store_sem.at[4]))
    stores[-1].start()

    weight_bytes = weight.at[pl.ds(0, 64 * (FRAMES - 1)), columns]
    remote(weight_bytes, weight_bytes, send_sem.at[0], recv_sem.at[0], partner).wait_send()
    view_bytes.wait_send()
    remote(
        own.at[3, pl.ds(0, others)], of_frame.at[3, pl.ds(0, others)], send_sem.at[2], recv_sem.at[2], partner
    ).wait_send()
    for half in range(2):
        rows_of_half(half, own, of_frame, 3 + half).wait_send()
        rows_of_half(half, frame_res, frame_back, 6 + half).wait_send()
    remote(
        view_res.at[:, pl.ds(0, 2 * (VIEWS - 1))], view_back.at[:, pl.ds(0, 2 * (VIEWS - 1))], send_sem.at[5],
        recv_sem.at[5], partner,
    ).wait_send()
    remote(
        frame_out.at[pl.ds(0, others)], frame_in.at[pl.ds(0, others)], send_sem.at[8], recv_sem.at[8], partner
    ).wait_send()
    for copy in slices + passes + to_core + to_chip + to_sample:
        copy.wait_send()
    for store in stores:
        store.wait()


def local(query_rows, key_rows, value_rows, cotangent, out_weight):
    shape = query_rows.shape
    tokens = (16, 8, D)
    rows = [array.reshape(tokens) for array in (query_rows, key_rows, value_rows, cotangent)]
    four = pltpu.VMEM((4,) + tokens, BF16)
    probs = pltpu.VMEM((PAIRS, 256, 128), F32)
    dma = pltpu.SemaphoreType.DMA
    out = jax.ShapeDtypeStruct(tokens, BF16)
    outs = pl.pallas_call(
        kernel,
        out_shape=(out, out, out, out, jax.ShapeDtypeStruct((8, D), BF16)),
        in_specs=[pl.BlockSpec(memory_space=pl.ANY)] * 5,
        out_specs=(pl.BlockSpec(memory_space=pl.ANY),) * 5,
        scratch_shapes=[
            four, four, four, pltpu.VMEM((64, D), BF16), pltpu.VMEM((D, D), BF16),
            four, four, four, four, four,
            probs, probs, pltpu.VMEM((128, D), BF16), pltpu.VMEM((384, D), BF16),
            four, four, four, four, pltpu.VMEM(tokens, BF16), pltpu.VMEM(tokens, BF16),
            pltpu.VMEM((8, D), F32), pltpu.VMEM((4, 8, D), F32),
            four, pltpu.VMEM((8, D), BF16),
            dma((5,)), dma((5,)), dma((9,)), dma((9,)), dma((8,)), dma((8,)), dma((4,)), dma((4,)),
            dma((4,)), dma((4,)), dma((4,)), dma((4,)),
        ],
        compiler_params=pltpu.CompilerParams(
            collective_id=0, has_side_effects=True, vmem_limit_bytes=52 * 2**20
        ),
        name="attention",
    )(*rows, out_weight)
    return tuple(array.reshape(shape) for array in outs[:4]) + (outs[4],)


def solution(mesh):
    tokens = P("dp", "view", "frame", None, None)
    return jax.shard_map(
        local,
        mesh=mesh,
        in_specs=(tokens, tokens, tokens, tokens, P("frame", None)),
        out_specs=(tokens, tokens, tokens, tokens, P(("view", "frame"), None)),
        check_vma=False,
    )
```

```python
import functools

import jax
import jax.numpy as jnp
from jax import lax
from jax.experimental import pallas as pl
from jax.experimental.pallas import tpu as pltpu
from jax.sharding import PartitionSpec as P

F32 = jnp.float32
BF16 = jnp.bfloat16
MESH = pl.DeviceIdType.MESH
NN = (((1,), (0,)), ((), ()))
NT = (((1,), (1,)), ((), ()))
TN = (((0,), (0,)), ((), ()))
MASKED = -1e30

D = 1024
VIEWS = 8
FRAMES = 16
CHIPS = VIEWS // 2
PAIRS = D // 128
HALF = D // 2
SCALE = 0.125


def dot(left, right, dims):
    return lax.dot_general(left, right, dims, preferred_element_type=F32)


def flat(block):
    return block.reshape(block.shape[0] * block.shape[1], block.shape[2])


def blocks(rows):
    return rows.reshape(rows.shape[0] // 8, 8, rows.shape[1])


def lower_lanes():
    return lax.broadcasted_iota(jnp.int32, (128, 128), 1) < 64


def by_head(rows, lower):
    one = lower.astype(F32).astype(BF16)
    other = (1.0 - lower.astype(F32)).astype(BF16)
    return jnp.concatenate([rows * one, rows * other], axis=0)


def group_bias(modulus):
    row = lax.broadcasted_iota(jnp.int32, (128, 128), 0)
    column = lax.broadcasted_iota(jnp.int32, (128, 128), 1)
    same = lax.rem(row, modulus) == lax.rem(column, modulus)
    return jnp.where(same, 0.0, MASKED).astype(F32)


def forward_pair(query, key, value, bias, lower):
    scores = dot(by_head(key, lower), query, NT) * SCALE
    halves = []
    for head in range(2):
        part = scores[128 * head : 128 * head + 128]
        if bias is not None:
            part = part + bias
        raised = jnp.exp(part - jnp.max(part, axis=0, keepdims=True))
        halves.append(raised * (1.0 / jnp.sum(raised, axis=0, keepdims=True)))
    probs = jnp.concatenate(halves, axis=0)
    out = dot(probs.astype(BF16), by_head(value, lower), TN)
    return probs, out


def backward_pair(query, key, value, grad, probs, lower):
    dprob = dot(by_head(value, lower), grad, NT)
    halves = []
    for head in range(2):
        prob = probs[128 * head : 128 * head + 128]
        term = prob * dprob[128 * head : 128 * head + 128]
        halves.append((term - prob * jnp.sum(term, axis=0, keepdims=True)).astype(BF16))
    dscore = jnp.concatenate(halves, axis=0)
    value_grad = dot(probs.astype(BF16), grad, NN)
    value_grad = jnp.where(lower, value_grad[:128], value_grad[128:])
    key_grad = dot(dscore, query, NN)
    key_grad = jnp.where(lower, key_grad[:128], key_grad[128:]) * SCALE
    query_grad = dot(dscore, by_head(key, lower), TN) * SCALE
    return query_grad, key_grad, value_grad


def frame_offset(step):
    far = lax.rem(step, 2)
    turn = step // 2
    odd = lax.rem(turn, 2)
    near = odd * ((turn + 1) // 2) + (1 - odd) * lax.rem(8 - turn // 2, 8)
    return near, far


def kernel(
    q_hbm, k_hbm, v_hbm, c_hbm, w_hbm,
    proj_hbm, dq_hbm, dk_hbm, dv_hbm, wg_hbm,
    own, of_view, of_frame, shard, weight,
    own_res, view_res, frame_res, view_back, frame_back,
    own_probs, view_probs, frame_probs, grad, frame_grad, rows,
    core_out, core_in, chip_out, chip_in, near_out, near_in, far_out, far_in,
    results, last,
    load_sem, store_sem, send_sem, recv_sem, core_send, core_recv, chip_send, chip_recv,
    slice_send, slice_recv, pass_send, pass_recv,
):
    sample = lax.axis_index("dp")
    view = lax.axis_index("view")
    frame = lax.axis_index("frame")
    chip = view // 2
    core = lax.rem(view, 2)
    far = frame // 8
    near = lax.rem(frame, 8)
    column = far * 4 + sample
    partner = {"view": chip * 2 + 1 - core}
    opposite = lax.rem(far + 1, 2) * 8 + near
    low = lax.rem(chip, 2)
    halves = (1 - chip // 2, chip // 2)
    others = FRAMES - 1

    def frame_peer(step):
        by, across = frame_offset(step)
        return lax.rem(far + across, 2) * 8 + lax.rem(near + by, 8)

    def near_peer(step):
        by, _ = frame_offset(step * 2)
        return lax.rem(near + by, 8)

    def view_peer(step):
        return lax.rem(view + step, VIEWS)

    def column_device(step):
        other = lax.rem(column + step, 8)
        return {"dp": lax.rem(other, 4), "frame": (other // 4) * 8 + near}, other

    def chip_peer(step):
        return lax.rem(chip + step, CHIPS)

    def chip_device(step):
        return {"view": chip_peer(step) * 2 + core}

    def remote(source, target, send, recv, device):
        return pltpu.make_async_remote_copy(
            src_ref=source, dst_ref=target, send_sem=send, recv_sem=recv,
            device_id=device, device_id_type=MESH,
        )

    def group(source, target, slot):
        return remote(source, target, send_sem.at[slot], recv_sem.at[slot], partner)

    def each(first, last_step, body):
        def step(index, carry):
            body(index)
            return carry

        lax.fori_loop(first, last_step, step, 0)

    with jax.named_scope("load_and_greet"):
        loads = [pltpu.make_async_copy(w_hbm, shard, load_sem.at[4])]
        for index, source in enumerate((q_hbm, k_hbm, v_hbm, c_hbm)):
            loads.append(pltpu.make_async_copy(source, own.at[index], load_sem.at[index]))
        for load in loads:
            load.start()
        barrier = pltpu.get_barrier_semaphore()

        def greet(device):
            pl.semaphore_signal(barrier, inc=1, device_id=device, device_id_type=MESH)

        each(1, FRAMES, lambda step: greet({"frame": frame_peer(step)}))
        each(1, VIEWS, lambda step: greet({"view": view_peer(step)}))
        each(1, 4, lambda step: greet(column_device(step)[0]))
        each(5, 8, lambda step: greet(column_device(step)[0]))
        pl.semaphore_wait(barrier, FRAMES - 1 + VIEWS - 1 + 6)
        for load in loads:
            load.wait()

    columns = pl.ds(pl.multiple_of(view * 128, 128), 128)

    def shard_rows(which):
        return pl.ds(pl.multiple_of(which * 64, 64), 64)

    across = remote(
        shard.at[:, columns], weight.at[shard_rows(frame), columns], slice_send.at[0], slice_recv.at[0],
        {"frame": opposite},
    )

    def send_weight(source, which, slot):
        def send(step):
            remote(
                source, weight.at[shard_rows(which), columns], send_sem.at[slot], recv_sem.at[slot],
                {"frame": far * 8 + near_peer(step)},
            ).start()

        return send

    def near_weight(slot):
        part = weight.at[pl.ds(0, 64 * 7), columns]
        return group(part, part, slot)

    def send_view(step):
        peer = view_peer(step)
        remote(
            own.at[:, pl.ds(peer * 2, 2)], of_view.at[:, pl.ds(view * 2, 2)], send_sem.at[1], recv_sem.at[1],
            {"view": peer},
        ).start()

    def view_group(source, target, first, count, slot):
        parts, most = pl.ds(first, count), pl.ds(0, 2 * (VIEWS - 1))
        return group(source.at[parts, most], target.at[parts, most], slot)

    def send_frame_grad(step):
        peer = frame_peer(step)
        remote(own.at[3, peer], of_frame.at[3, frame], send_sem.at[2], recv_sem.at[2], {"frame": peer}).start()

    def frame_group(source, target, first, count, lanes, slot):
        parts, most = pl.ds(first, count), pl.ds(0, others)
        return group(source.at[parts, most, :, lanes], target.at[parts, most, :, lanes], slot)

    def lanes_of_half(half):
        return pl.ds(pl.multiple_of(halves[half] * HALF, HALF), HALF)

    def send_frame_rows(half):
        lanes = lanes_of_half(half)

        def send(step):
            peer = frame_peer(step)
            remote(
                own.at[pl.ds(0, 3), peer, :, lanes], of_frame.at[pl.ds(0, 3), frame, :, lanes],
                send_sem.at[3 + half], recv_sem.at[3 + half], {"frame": peer},
            ).start()

        return send

    with jax.named_scope("send_first"):
        across.start()
        each(1, 8, send_weight(shard.at[:, columns], frame, 0))
        each(1, VIEWS, send_view)
        weight[shard_rows(frame), columns] = shard[:, columns]
        of_frame[:, pl.ds(frame, 1)] = own[:, pl.ds(frame, 1)]
        of_view[:, pl.ds(view * 2, 2)] = own[:, pl.ds(view * 2, 2)]

    lower = lower_lanes()

    def lanes_of(pair):
        return pl.ds(pl.multiple_of(pair * 128, 128), 128)

    def forward(source, target, kept, bias, first=0, count=PAIRS):
        def step(pair):
            lanes = lanes_of(pair)
            query, key, value = (flat(source[index, :, :, lanes]) for index in range(3))
            probs, out = forward_pair(query, key, value, bias, lower)
            kept[pair] = probs
            target[0, :, :, lanes] = blocks(out.astype(BF16))

        def two(index):
            step(first + index * 2)
            step(first + index * 2 + 1)

        each(0, count // 2, two)

    def grad_rows(source, target):
        cotangent = flat(source[3])
        for part in range(4):
            wide = slice(256 * part, 256 * part + 256)
            target[:, wide] = dot(cotangent, weight[wide, :], NT).astype(BF16)

    def backward(source, target, kept, grad, first=0, count=PAIRS):
        def step(pair):
            lanes = lanes_of(pair)
            query, key, value = (flat(source[index, :, :, lanes]) for index in range(3))
            grads = backward_pair(query, key, value, grad[:, lanes], kept[pair], lower)
            for index, term in enumerate(grads):
                target[1 + index, :, :, lanes] = blocks(term.astype(BF16))

        def two(index):
            step(first + index * 2)
            step(first + index * 2 + 1)

        each(0, count // 2, two)

    with jax.named_scope("spatial_forward"):
        forward(own, own_res, own_probs, None, 0, PAIRS // 2)
    with jax.named_scope("wait_weight_opposite"):
        across.wait_recv()
    with jax.named_scope("send_weight"):
        each(1, 8, send_weight(weight.at[shard_rows(opposite), columns], opposite, 10))
    with jax.named_scope("spatial_forward"):
        forward(own, own_res, own_probs, None, PAIRS // 2, PAIRS // 2)
    with jax.named_scope("send_frames"):
        each(1, FRAMES, send_frame_rows(0))
        each(1, FRAMES, send_frame_grad)
        each(1, FRAMES, send_frame_rows(1))

    with jax.named_scope("wait_weight_frames"):
        near_weight(0).wait_recv()
        near_weight(10).wait_recv()
    def slice_of(step, first, count):
        came = chip_peer(CHIPS - step) * 2 + core
        return weight.at[pl.ds(first, count), pl.ds(pl.multiple_of(came * 128, 128), 128)]

    def along(step, first, count, index, to):
        part = slice_of(step, first, count)
        copy = remote(part, part, slice_send.at[index], slice_recv.at[index], chip_device(to))
        copy.start()
        return copy

    def to_partner(step, first, count, index):
        part = slice_of(step, first, count)
        copy = remote(part, part, pass_send.at[index], pass_recv.at[index], partner)
        copy.start()
        return copy

    with jax.named_scope("pass_weight"):
        slices = [along(0, 0, D, 1, 1), along(0, 0, D, 3, 3)]
        passes = [to_partner(0, 0, D, 0)]

    with jax.named_scope("wait_view_rows"):
        view_group(own, of_view, 0, 4, 1).wait_recv()
    with jax.named_scope("view_forward"):
        forward(of_view, view_res, view_probs, group_bias(16))

    with jax.named_scope("wait_weight_chips"):
        slices[0].wait_recv()
        slices.append(along(1, 0, HALF, 2, 1))
        slices[1].wait_recv()
        slices.append(along(3, HALF, HALF, 4, 3))
        passes.append(to_partner(1, 0, D, 1))
        passes.append(to_partner(3, 0, D, 3))
    def return_view():
        def send(step):
            peer = view_peer(step)
            remote(
                view_res.at[:, pl.ds(peer * 2, 2)], view_back.at[:, pl.ds(view * 2, 2)],
                send_sem.at[5], recv_sem.at[5], {"view": peer},
            ).start()

        each(1, VIEWS, send)
        view_back[:, pl.ds(view * 2, 2)] = view_res[:, pl.ds(view * 2, 2)]

    def return_frame(half, first, count, slot):
        lanes = lanes_of_half(half)
        parts = pl.ds(first, count)

        def send(step):
            peer = frame_peer(step)
            remote(
                frame_res.at[parts, peer, :, lanes], frame_back.at[parts, frame, :, lanes],
                send_sem.at[slot], recv_sem.at[slot], {"frame": peer},
            ).start()

        each(1, FRAMES, send)
        for index in range(first, first + count):
            frame_back[index, pl.ds(frame, 1), :, lanes] = frame_res[index, pl.ds(frame, 1), :, lanes]

    everything = pl.ds(0, D)
    frame_bias = group_bias(8)

    def frame_forward(half):
        with jax.named_scope("wait_frame_rows"):
            frame_group(own, of_frame, 0, 3, lanes_of_half(half), 3 + half).wait_recv()
        with jax.named_scope("frame_forward"):
            forward(of_frame, frame_res, frame_probs, frame_bias, halves[half] * (PAIRS // 2), PAIRS // 2)

    def frame_backward(half):
        with jax.named_scope("frame_backward"):
            backward(of_frame, frame_res, frame_probs, frame_grad, halves[half] * (PAIRS // 2), PAIRS // 2)

    targets = (halves[0] * 2 + low, halves[0] * 2 + 1 - low, halves[1] * 2 + 1 - low, chip)

    def gradient_rows(which):
        lanes = lanes_of(which)
        left = jnp.concatenate(
            [flat(res[0, :, :, lanes]) for res in (own_res, view_res, frame_res)], axis=0
        )
        return [dot(left, rows[:, HALF * part : HALF * part + HALF], TN) for part in range(2)]

    to_core, to_chip = [], []

    def gradient_to_chips(half):
        with jax.named_scope("gradient_to_core"):
            for slot in (2 * half, 2 * half + 1):
                for part, value in enumerate(gradient_rows(targets[slot] * 2 + 1 - core)):
                    core_out[slot, :, :, HALF * part : HALF * part + HALF] = blocks(value.astype(BF16))
                copy = remote(core_out.at[slot], core_in.at[slot], core_send.at[slot], core_recv.at[slot], partner)
                copy.start()
                to_core.append(copy)
        with jax.named_scope("gradient_to_chips"):
            for slot in (2 * half, 2 * half + 1):
                values = gradient_rows(targets[slot] * 2 + core)
                to_core[slot].wait_recv()
                for part, value in enumerate(values):
                    wide = slice(HALF * part, HALF * part + HALF)
                    total = value + flat(core_in[slot, :, :, wide]).astype(F32)
                    chip_out[slot, :, :, wide] = blocks(total.astype(BF16))
                if slot < 3:
                    copy = remote(
                        chip_out.at[slot], chip_in.at[slot], chip_send.at[slot], chip_recv.at[slot],
                        {"view": targets[slot] * 2 + core},
                    )
                    copy.start()
                    to_chip.append(copy)

    frame_forward(0)
    with jax.named_scope("wait_weight_chips"):
        slices[2].wait_recv()
        passes.append(to_partner(2, 0, HALF, 2))
        slices[3].wait_recv()
        passes.append(to_partner(2, HALF, HALF, 4))

    with jax.named_scope("wait_frame_cotangent"):
        frame_group(own, of_frame, 3, 1, everything, 2).wait_recv()
    for index, source in enumerate((own, of_view, of_frame)):
        rows[128 * index : 128 * index + 128] = flat(source[3])
    gradient_to_chips(0)
    with jax.named_scope("wait_weight_core"):
        for onward in passes:
            onward.wait_recv()
    with jax.named_scope("frame_grad"):
        grad_rows(of_frame, frame_grad)
    frame_backward(0)
    with jax.named_scope("return_frame"):
        return_frame(0, 0, 4, 6)

    frame_forward(1)
    gradient_to_chips(1)
    frame_backward(1)
    with jax.named_scope("return_frame"):
        return_frame(1, 0, 2, 7)

    with jax.named_scope("view_backward"):
        grad_rows(of_view, grad)
        backward(of_view, view_res, view_probs, grad)
    with jax.named_scope("return_view"):
        return_view()

    def gradient_near():
        most = pl.ds(0, 7)
        return group(near_out.at[:, most], near_in.at[:, most], 8)

    def gradient_far():
        part = far_in.at[pl.ds(0, 7)]
        return group(part, part, 9)

    def send_near(step):
        peer = near_peer(step)
        remote(
            near_out.at[:, peer], near_in.at[:, near], send_sem.at[8], recv_sem.at[8], {"frame": far * 8 + peer}
        ).start()

    def send_far(step):
        device, other = column_device(step)
        remote(far_out.at[other // 4], far_in.at[column], send_sem.at[9], recv_sem.at[9], device).start()

    with jax.named_scope("wait_gradient_chips"):
        for copy in to_chip:
            copy.wait_recv()
    with jax.named_scope("gradient_to_near"):
        for part in range(4):
            wide = slice(256 * part, 256 * part + 256)
            total = chip_out[3, :, :, wide].astype(F32)
            for slot in range(3):
                total = total + chip_in[slot, :, :, wide].astype(F32)
            for index in range(2):
                near_out[index, :, :, wide] = total[8 * index : 8 * index + 8].astype(BF16)
        each(1, 8, send_near)
        near_in[:, pl.ds(near, 1)] = near_out[:, pl.ds(near, 1)]

    with jax.named_scope("spatial_backward"):
        grad_rows(own, grad)
        backward(own, own_res, own_probs, grad)
    with jax.named_scope("return_frame"):
        return_frame(1, 2, 2, 11)

    with jax.named_scope("wait_gradient_near"):
        gradient_near().wait_recv()
    with jax.named_scope("gradient_to_far"):
        for index in range(2):
            total = near_in[index, 0].astype(F32)
            for peer in range(1, 8):
                total = total + near_in[index, peer].astype(F32)
            far_out[index] = total.astype(BF16)
        each(1, 8, send_far)
        far_in[pl.ds(column, 1)] = far_out[pl.ds(far, 1)]

    def add_terms(index, lanes):
        total = own_res[index, :, :, lanes].astype(F32) + view_back[index, :, :, lanes].astype(F32)
        total = total + frame_back[index, :, :, lanes].astype(F32)
        results[index, :, :, lanes] = total.astype(BF16)

    stores = []

    def put(source, target, slot):
        stores.append(pltpu.make_async_copy(source, target, store_sem.at[slot]))
        stores[-1].start()

    def columns_of(half, part):
        return pl.ds(pl.multiple_of(halves[half] * HALF + 256 * part, 256), 256)

    with jax.named_scope("wait_view_back"):
        view_group(view_res, view_back, 0, 4, 5).wait_recv()
    with jax.named_scope("wait_frame_back"):
        frame_group(frame_res, frame_back, 0, 4, lanes_of_half(0), 6).wait_recv()
    with jax.named_scope("add_terms"):
        for index in range(4):
            for part in range(2):
                add_terms(index, columns_of(0, part))

    with jax.named_scope("wait_frame_back"):
        frame_group(frame_res, frame_back, 0, 2, lanes_of_half(1), 7).wait_recv()
    with jax.named_scope("add_terms"):
        for index in range(2):
            for part in range(2):
                add_terms(index, columns_of(1, part))
    put(results.at[1], dq_hbm, 1)
    with jax.named_scope("project"):
        attended = flat(results[0])
        for part in range(4):
            wide = slice(256 * part, 256 * part + 256)
            own_res[0, :, :, wide] = blocks(dot(attended, weight[:, wide], NN).astype(BF16))
        put(own_res.at[0], proj_hbm, 0)

    with jax.named_scope("wait_frame_back"):
        frame_group(frame_res, frame_back, 2, 2, lanes_of_half(1), 11).wait_recv()
    with jax.named_scope("add_terms"):
        for index in range(2, 4):
            for part in range(2):
                add_terms(index, columns_of(1, part))
    put(results.at[2], dk_hbm, 2)
    put(results.at[3], dv_hbm, 3)

    with jax.named_scope("wait_gradient_far"):
        gradient_far().wait_recv()
    total = far_in[0].astype(F32)
    for index in range(1, 8):
        total = total + far_in[index].astype(F32)
    last[...] = (total * (1.0 / 256.0)).astype(BF16)
    put(last, wg_hbm, 4)

    with jax.named_scope("drain"):
        near_weight(0).wait_send()
        near_weight(10).wait_send()
        across.wait_send()
        view_group(own, of_view, 0, 4, 1).wait_send()
        view_group(view_res, view_back, 0, 4, 5).wait_send()
        frame_group(own, of_frame, 3, 1, everything, 2).wait_send()
        for half in range(2):
            frame_group(own, of_frame, 0, 3, lanes_of_half(half), 3 + half).wait_send()
        frame_group(frame_res, frame_back, 0, 4, lanes_of_half(0), 6).wait_send()
        frame_group(frame_res, frame_back, 0, 2, lanes_of_half(1), 7).wait_send()
        frame_group(frame_res, frame_back, 2, 2, lanes_of_half(1), 11).wait_send()
        gradient_far().wait_send()
        gradient_near().wait_send()
        for copy in slices + passes + to_core + to_chip:
            copy.wait_send()
        for copy in stores:
            copy.wait()


def store(*refs):
    copies = [pltpu.make_async_copy(refs[index], refs[5 + index], refs[10].at[index]) for index in range(5)]
    for copy in copies:
        copy.start()
    for copy in copies:
        copy.wait()


def local(query_rows, key_rows, value_rows, cotangent, out_weight):
    shape = query_rows.shape
    tokens = (16, 8, D)
    rows = [array.reshape(tokens) for array in (query_rows, key_rows, value_rows, cotangent)]
    rows = [pltpu.with_memory_space_constraint(array, pltpu.HBM) for array in rows + [out_weight]]
    four = pltpu.VMEM((4,) + tokens, BF16)
    near = pltpu.VMEM((2, 8, 8, D), BF16)
    probs = pltpu.VMEM((PAIRS, 256, 128), F32)
    dma = pltpu.SemaphoreType.DMA
    out = jax.ShapeDtypeStruct(tokens, BF16)
    outs = pl.pallas_call(
        kernel,
        out_shape=(out, out, out, out, jax.ShapeDtypeStruct((8, D), BF16)),
        in_specs=[pl.BlockSpec(memory_space=pltpu.HBM)] * 5,
        out_specs=(pl.BlockSpec(memory_space=pl.ANY),) * 5,
        scratch_shapes=[
            four, four, four, pltpu.VMEM((64, D), BF16), pltpu.VMEM((D, D), BF16),
            four, four, four, four, four,
            probs, probs, probs, pltpu.VMEM((128, D), BF16), pltpu.VMEM((128, D), BF16), pltpu.VMEM((384, D), BF16),
            four, four, four, four, near, near, pltpu.VMEM((2, 8, D), BF16), pltpu.VMEM((8, 8, D), BF16),
            four, pltpu.VMEM((8, D), BF16),
            dma((5,)), dma((5,)), dma((13,)), dma((13,)), dma((4,)), dma((4,)), dma((4,)), dma((4,)),
            dma((5,)), dma((5,)), dma((5,)), dma((5,)),
        ],
        compiler_params=pltpu.CompilerParams(
            collective_id=0, has_side_effects=True, vmem_limit_bytes=52 * 2**20
        ),
        name="attention",
    )(*rows)
    outs = pl.pallas_call(
        store,
        out_shape=tuple(jax.ShapeDtypeStruct(array.shape, BF16) for array in outs),
        in_specs=[pl.BlockSpec(memory_space=pl.ANY)] * 5,
        out_specs=(pl.BlockSpec(memory_space=pltpu.HBM),) * 5,
        scratch_shapes=[dma((5,))],
        compiler_params=pltpu.CompilerParams(vmem_limit_bytes=2**20),
        name="store",
    )(*outs)
    return tuple(array.reshape(shape) for array in outs[:4]) + (outs[4],)


def solution(mesh):
    tokens = P("dp", "view", "frame", None, None)
    return jax.shard_map(
        local,
        mesh=mesh,
        in_specs=(tokens, tokens, tokens, tokens, P("frame", None)),
        out_specs=(tokens, tokens, tokens, tokens, P(("view", "frame"), None)),
        check_vma=False,
    )
```

```python
import functools

import jax
import jax.numpy as jnp
from jax import lax
from jax.experimental import pallas as pl
from jax.experimental.pallas import tpu as pltpu
from jax.sharding import PartitionSpec as P

F32 = jnp.float32
BF16 = jnp.bfloat16
MESH = pl.DeviceIdType.MESH
NN = (((1,), (0,)), ((), ()))
NT = (((1,), (1,)), ((), ()))
TN = (((0,), (0,)), ((), ()))
MASKED = -1e30

D = 1024
VIEWS = 8
FRAMES = 16
CHIPS = VIEWS // 2
PAIRS = D // 128
HALF = D // 2
SCALE = 0.125


def dot(left, right, dims):
    return lax.dot_general(left, right, dims, preferred_element_type=F32)


def flat(block):
    return block.reshape(block.shape[0] * block.shape[1], block.shape[2])


def blocks(rows):
    return rows.reshape(rows.shape[0] // 8, 8, rows.shape[1])


def lower_lanes():
    return lax.broadcasted_iota(jnp.int32, (128, 128), 1) < 64


def by_head(rows, lower):
    one = lower.astype(F32).astype(BF16)
    other = (1.0 - lower.astype(F32)).astype(BF16)
    return jnp.concatenate([rows * one, rows * other], axis=0)


def group_bias(modulus):
    row = lax.broadcasted_iota(jnp.int32, (128, 128), 0)
    column = lax.broadcasted_iota(jnp.int32, (128, 128), 1)
    same = lax.rem(row, modulus) == lax.rem(column, modulus)
    return jnp.where(same, 0.0, MASKED).astype(F32)


def forward_pair(query, key, value, bias, lower):
    scores = dot(by_head(key, lower), query, NT) * SCALE
    halves = []
    for head in range(2):
        part = scores[128 * head : 128 * head + 128]
        if bias is not None:
            part = part + bias
        raised = jnp.exp(part - jnp.max(part, axis=0, keepdims=True))
        halves.append(raised * (1.0 / jnp.sum(raised, axis=0, keepdims=True)))
    probs = jnp.concatenate(halves, axis=0)
    out = dot(probs.astype(BF16), by_head(value, lower), TN)
    return probs, out


def backward_pair(query, key, value, grad, probs, lower):
    dprob = dot(by_head(value, lower), grad, NT)
    halves = []
    for head in range(2):
        prob = probs[128 * head : 128 * head + 128]
        term = prob * dprob[128 * head : 128 * head + 128]
        halves.append((term - prob * jnp.sum(term, axis=0, keepdims=True)).astype(BF16))
    dscore = jnp.concatenate(halves, axis=0)
    value_grad = dot(probs.astype(BF16), grad, NN)
    value_grad = jnp.where(lower, value_grad[:128], value_grad[128:])
    key_grad = dot(dscore, query, NN)
    key_grad = jnp.where(lower, key_grad[:128], key_grad[128:]) * SCALE
    query_grad = dot(dscore, by_head(key, lower), TN) * SCALE
    return query_grad, key_grad, value_grad


def frame_offset(step):
    far = lax.rem(step, 2)
    turn = step // 2
    odd = lax.rem(turn, 2)
    near = odd * ((turn + 1) // 2) + (1 - odd) * lax.rem(8 - turn // 2, 8)
    return near, far


def kernel(
    q_hbm, k_hbm, v_hbm, c_hbm, w_hbm,
    proj_hbm, dq_hbm, dk_hbm, dv_hbm, wg_hbm,
    own, of_view, of_frame, shard, weight,
    own_res, view_res, frame_res, view_back, frame_back,
    own_probs, view_probs, frame_probs, grad, frame_grad, rows,
    core_out, core_in, chip_out, chip_in, near_out, near_in, far_out, far_in,
    results, last,
    load_sem, store_sem, send_sem, recv_sem, core_send, core_recv, chip_send, chip_recv,
    slice_send, slice_recv, pass_send, pass_recv,
):
    sample = lax.axis_index("dp")
    view = lax.axis_index("view")
    frame = lax.axis_index("frame")
    chip = view // 2
    core = lax.rem(view, 2)
    far = frame // 8
    near = lax.rem(frame, 8)
    column = far * 4 + sample
    partner = {"view": chip * 2 + 1 - core}
    opposite = lax.rem(far + 1, 2) * 8 + near
    low = lax.rem(chip, 2)
    halves = (1 - chip // 2, chip // 2)
    others = FRAMES - 1

    def frame_peer(step):
        by, across = frame_offset(step)
        return lax.rem(far + across, 2) * 8 + lax.rem(near + by, 8)

    def near_peer(step):
        by, _ = frame_offset(step * 2)
        return lax.rem(near + by, 8)

    def view_peer(step):
        return lax.rem(view + step, VIEWS)

    def column_device(step):
        other = lax.rem(column + step, 8)
        return {"dp": lax.rem(other, 4), "frame": (other // 4) * 8 + near}, other

    def chip_peer(step):
        return lax.rem(chip + step, CHIPS)

    def chip_device(step):
        return {"view": chip_peer(step) * 2 + core}

    def remote(source, target, send, recv, device):
        return pltpu.make_async_remote_copy(
            src_ref=source, dst_ref=target, send_sem=send, recv_sem=recv,
            device_id=device, device_id_type=MESH,
        )

    def group(source, target, slot):
        return remote(source, target, send_sem.at[slot], recv_sem.at[slot], partner)

    def each(first, last_step, body):
        def step(index, carry):
            body(index)
            return carry

        lax.fori_loop(first, last_step, step, 0)

    with jax.named_scope("load_and_greet"):
        loads = [pltpu.make_async_copy(w_hbm, shard, load_sem.at[4])]
        for index, source in enumerate((q_hbm, k_hbm, v_hbm, c_hbm)):
            loads.append(pltpu.make_async_copy(source, own.at[index], load_sem.at[index]))
        for load in loads:
            load.start()
        barrier = pltpu.get_barrier_semaphore()

        def greet(device):
            pl.semaphore_signal(barrier, inc=1, device_id=device, device_id_type=MESH)

        each(1, FRAMES, lambda step: greet({"frame": frame_peer(step)}))
        each(1, VIEWS, lambda step: greet({"view": view_peer(step)}))
        each(1, 4, lambda step: greet(column_device(step)[0]))
        each(5, 8, lambda step: greet(column_device(step)[0]))
        pl.semaphore_wait(barrier, FRAMES - 1 + VIEWS - 1 + 6)
        for load in loads:
            load.wait()

    columns = pl.ds(pl.multiple_of(view * 128, 128), 128)

    def shard_rows(which):
        return pl.ds(pl.multiple_of(which * 64, 64), 64)

    across = remote(
        shard.at[:, columns], weight.at[shard_rows(frame), columns], slice_send.at[0], slice_recv.at[0],
        {"frame": opposite},
    )

    def send_weight(source, which, slot):
        def send(step):
            remote(
                source, weight.at[shard_rows(which), columns], send_sem.at[slot], recv_sem.at[slot],
                {"frame": far * 8 + near_peer(step)},
            ).start()

        return send

    def near_weight(slot):
        part = weight.at[pl.ds(0, 64 * 7), columns]
        return group(part, part, slot)

    def send_view(step):
        peer = view_peer(step)
        remote(
            own.at[:, pl.ds(peer * 2, 2)], of_view.at[:, pl.ds(view * 2, 2)], send_sem.at[1], recv_sem.at[1],
            {"view": peer},
        ).start()

    def view_group(source, target, first, count, slot):
        parts, most = pl.ds(first, count), pl.ds(0, 2 * (VIEWS - 1))
        return group(source.at[parts, most], target.at[parts, most], slot)

    def send_frame_grad(step):
        peer = frame_peer(step)
        remote(own.at[3, peer], of_frame.at[3, frame], send_sem.at[2], recv_sem.at[2], {"frame": peer}).start()

    def frame_group(source, target, first, count, lanes, slot):
        parts, most = pl.ds(first, count), pl.ds(0, others)
        return group(source.at[parts, most, :, lanes], target.at[parts, most, :, lanes], slot)

    def lanes_of_half(half):
        return pl.ds(pl.multiple_of(halves[half] * HALF, HALF), HALF)

    def send_frame_rows(half):
        lanes = lanes_of_half(half)

        def send(step):
            peer = frame_peer(step)
            remote(
                own.at[pl.ds(0, 3), peer, :, lanes], of_frame.at[pl.ds(0, 3), frame, :, lanes],
                send_sem.at[3 + half], recv_sem.at[3 + half], {"frame": peer},
            ).start()

        return send

    with jax.named_scope("send_first"):
        across.start()
        each(1, 8, send_weight(shard.at[:, columns], frame, 0))
        each(1, FRAMES, send_frame_grad)
        each(1, VIEWS, send_view)
        weight[shard_rows(frame), columns] = shard[:, columns]
        of_frame[:, pl.ds(frame, 1)] = own[:, pl.ds(frame, 1)]
        of_view[:, pl.ds(view * 2, 2)] = own[:, pl.ds(view * 2, 2)]

    lower = lower_lanes()

    def lanes_of(pair):
        return pl.ds(pl.multiple_of(pair * 128, 128), 128)

    def forward(source, target, kept, bias, first=0, count=PAIRS):
        def step(pair):
            lanes = lanes_of(pair)
            query, key, value = (flat(source[index, :, :, lanes]) for index in range(3))
            probs, out = forward_pair(query, key, value, bias, lower)
            kept[pair] = probs
            target[0, :, :, lanes] = blocks(out.astype(BF16))

        def two(index):
            step(first + index * 2)
            step(first + index * 2 + 1)

        each(0, count // 2, two)

    def grad_rows(source, target):
        cotangent = flat(source[3])
        for part in range(4):
            wide = slice(256 * part, 256 * part + 256)
            target[:, wide] = dot(cotangent, weight[wide, :], NT).astype(BF16)

    def backward(source, target, kept, grad, first=0, count=PAIRS):
        def step(pair):
            lanes = lanes_of(pair)
            query, key, value = (flat(source[index, :, :, lanes]) for index in range(3))
            grads = backward_pair(query, key, value, grad[:, lanes], kept[pair], lower)
            for index, term in enumerate(grads):
                target[1 + index, :, :, lanes] = blocks(term.astype(BF16))

        def two(index):
            step(first + index * 2)
            step(first + index * 2 + 1)

        each(0, count // 2, two)

    with jax.named_scope("spatial_forward"):
        forward(own, own_res, own_probs, None, 0, PAIRS // 2)
    with jax.named_scope("wait_weight_opposite"):
        across.wait_recv()
    with jax.named_scope("send_weight"):
        each(1, 8, send_weight(weight.at[shard_rows(opposite), columns], opposite, 10))
    with jax.named_scope("spatial_forward"):
        forward(own, own_res, own_probs, None, PAIRS // 2, PAIRS // 2)
    with jax.named_scope("send_frames"):
        each(1, FRAMES, send_frame_rows(0))

    with jax.named_scope("wait_weight_frames"):
        near_weight(0).wait_recv()
        near_weight(10).wait_recv()
    def slice_of(step, first, count):
        came = chip_peer(CHIPS - step) * 2 + core
        return weight.at[pl.ds(first, count), pl.ds(pl.multiple_of(came * 128, 128), 128)]

    def along(step, first, count, index, to):
        part = slice_of(step, first, count)
        copy = remote(part, part, slice_send.at[index], slice_recv.at[index], chip_device(to))
        copy.start()
        return copy

    def to_partner(step, first, count, index):
        part = slice_of(step, first, count)
        copy = remote(part, part, pass_send.at[index], pass_recv.at[index], partner)
        copy.start()
        return copy

    with jax.named_scope("pass_weight"):
        slices = [along(0, 0, D, 1, 1), along(0, 0, D, 3, 3)]
        passes = [to_partner(0, 0, D, 0)]

    with jax.named_scope("wait_view_rows"):
        view_group(own, of_view, 0, 4, 1).wait_recv()
    with jax.named_scope("view_forward"):
        forward(of_view, view_res, view_probs, group_bias(16))
    with jax.named_scope("send_frames"):
        each(1, FRAMES, send_frame_rows(1))

    with jax.named_scope("wait_weight_chips"):
        slices[0].wait_recv()
        slices.append(along(1, 0, HALF, 2, 1))
        slices[1].wait_recv()
        slices.append(along(3, HALF, HALF, 4, 3))
        passes.append(to_partner(1, 0, D, 1))
        passes.append(to_partner(3, 0, D, 3))
    def return_view():
        def send(step):
            peer = view_peer(step)
            remote(
                view_res.at[:, pl.ds(peer * 2, 2)], view_back.at[:, pl.ds(view * 2, 2)],
                send_sem.at[5], recv_sem.at[5], {"view": peer},
            ).start()

        each(1, VIEWS, send)
        view_back[:, pl.ds(view * 2, 2)] = view_res[:, pl.ds(view * 2, 2)]

    def return_frame(half, first, count, slot):
        lanes = lanes_of_half(half)
        parts = pl.ds(first, count)

        def send(step):
            peer = frame_peer(step)
            remote(
                frame_res.at[parts, peer, :, lanes], frame_back.at[parts, frame, :, lanes],
                send_sem.at[slot], recv_sem.at[slot], {"frame": peer},
            ).start()

        each(1, FRAMES, send)
        for index in range(first, first + count):
            frame_back[index, pl.ds(frame, 1), :, lanes] = frame_res[index, pl.ds(frame, 1), :, lanes]

    everything = pl.ds(0, D)
    frame_bias = group_bias(8)

    def frame_forward(half):
        with jax.named_scope("wait_frame_rows"):
            frame_group(own, of_frame, 0, 3, lanes_of_half(half), 3 + half).wait_recv()
        with jax.named_scope("frame_forward"):
            forward(of_frame, frame_res, frame_probs, frame_bias, halves[half] * (PAIRS // 2), PAIRS // 2)

    def frame_backward(half):
        with jax.named_scope("frame_backward"):
            backward(of_frame, frame_res, frame_probs, frame_grad, halves[half] * (PAIRS // 2), PAIRS // 2)

    targets = (halves[0] * 2 + low, halves[0] * 2 + 1 - low, halves[1] * 2 + 1 - low, chip)

    def gradient_rows(which):
        lanes = lanes_of(which)
        left = jnp.concatenate(
            [flat(res[0, :, :, lanes]) for res in (own_res, view_res, frame_res)], axis=0
        )
        return [dot(left, rows[:, HALF * part : HALF * part + HALF], TN) for part in range(2)]

    to_core, to_chip = [], []

    def gradient_to_chips(half):
        with jax.named_scope("gradient_to_core"):
            for slot in (2 * half, 2 * half + 1):
                for part, value in enumerate(gradient_rows(targets[slot] * 2 + 1 - core)):
                    core_out[slot, :, :, HALF * part : HALF * part + HALF] = blocks(value.astype(BF16))
                copy = remote(core_out.at[slot], core_in.at[slot], core_send.at[slot], core_recv.at[slot], partner)
                copy.start()
                to_core.append(copy)
        with jax.named_scope("gradient_to_chips"):
            for slot in (2 * half, 2 * half + 1):
                values = gradient_rows(targets[slot] * 2 + core)
                to_core[slot].wait_recv()
                for part, value in enumerate(values):
                    wide = slice(HALF * part, HALF * part + HALF)
                    total = value + flat(core_in[slot, :, :, wide]).astype(F32)
                    chip_out[slot, :, :, wide] = blocks(total.astype(BF16))
                if slot < 3:
                    copy = remote(
                        chip_out.at[slot], chip_in.at[slot], chip_send.at[slot], chip_recv.at[slot],
                        {"view": targets[slot] * 2 + core},
                    )
                    copy.start()
                    to_chip.append(copy)

    with jax.named_scope("wait_weight_chips"):
        slices[2].wait_recv()
        passes.append(to_partner(2, 0, HALF, 2))
        slices[3].wait_recv()
        passes.append(to_partner(2, HALF, HALF, 4))

    frame_forward(0)
    with jax.named_scope("return_frame_out"):
        return_frame(0, 0, 1, 6)
    with jax.named_scope("wait_frame_cotangent"):
        frame_group(own, of_frame, 3, 1, everything, 2).wait_recv()
    with jax.named_scope("wait_weight_core"):
        for onward in passes:
            onward.wait_recv()
    with jax.named_scope("frame_grad"):
        grad_rows(of_frame, frame_grad)
    frame_backward(0)
    with jax.named_scope("return_frame"):
        return_frame(0, 1, 3, 13)
    for index, source in enumerate((own, of_view, of_frame)):
        rows[128 * index : 128 * index + 128] = flat(source[3])
    gradient_to_chips(0)

    frame_forward(1)
    with jax.named_scope("return_frame_out"):
        return_frame(1, 0, 1, 7)
    gradient_to_chips(1)
    frame_backward(1)
    with jax.named_scope("return_frame"):
        return_frame(1, 1, 1, 14)

    with jax.named_scope("view_backward"):
        grad_rows(of_view, grad)
        backward(of_view, view_res, view_probs, grad)
    with jax.named_scope("return_view"):
        return_view()

    def gradient_near():
        most = pl.ds(0, 7)
        return group(near_out.at[:, most], near_in.at[:, most], 8)

    def gradient_far():
        part = far_in.at[pl.ds(0, 7)]
        return group(part, part, 9)

    def send_near(step):
        peer = near_peer(step)
        remote(
            near_out.at[:, peer], near_in.at[:, near], send_sem.at[8], recv_sem.at[8], {"frame": far * 8 + peer}
        ).start()

    def send_far(step):
        device, other = column_device(step)
        remote(far_out.at[other // 4], far_in.at[column], send_sem.at[9], recv_sem.at[9], device).start()

    with jax.named_scope("wait_gradient_chips"):
        for copy in to_chip:
            copy.wait_recv()
    with jax.named_scope("gradient_to_near"):
        for part in range(4):
            wide = slice(256 * part, 256 * part + 256)
            total = chip_out[3, :, :, wide].astype(F32)
            for slot in range(3):
                total = total + chip_in[slot, :, :, wide].astype(F32)
            for index in range(2):
                near_out[index, :, :, wide] = total[8 * index : 8 * index + 8].astype(BF16)
        each(1, 8, send_near)
        near_in[:, pl.ds(near, 1)] = near_out[:, pl.ds(near, 1)]

    with jax.named_scope("return_frame"):
        return_frame(1, 2, 2, 11)

    with jax.named_scope("spatial_backward"):
        grad_rows(own, grad)
        backward(own, own_res, own_probs, grad)
    with jax.named_scope("wait_gradient_near"):
        gradient_near().wait_recv()
    with jax.named_scope("gradient_to_far"):
        for index in range(2):
            total = near_in[index, 0].astype(F32)
            for peer in range(1, 8):
                total = total + near_in[index, peer].astype(F32)
            far_out[index] = total.astype(BF16)
        each(1, 8, send_far)
        far_in[pl.ds(column, 1)] = far_out[pl.ds(far, 1)]

    def add_terms(index, lanes):
        total = own_res[index, :, :, lanes].astype(F32) + view_back[index, :, :, lanes].astype(F32)
        total = total + frame_back[index, :, :, lanes].astype(F32)
        results[index, :, :, lanes] = total.astype(BF16)

    stores = []

    def put(source, target, slot):
        stores.append(pltpu.make_async_copy(source, target, store_sem.at[slot]))
        stores[-1].start()

    def columns_of(half, part):
        return pl.ds(pl.multiple_of(halves[half] * HALF + 256 * part, 256), 256)

    with jax.named_scope("wait_view_back"):
        view_group(view_res, view_back, 0, 4, 5).wait_recv()
    with jax.named_scope("wait_frame_back"):
        frame_group(frame_res, frame_back, 0, 1, lanes_of_half(0), 6).wait_recv()
        frame_group(frame_res, frame_back, 1, 3, lanes_of_half(0), 13).wait_recv()
    with jax.named_scope("add_terms"):
        for index in range(4):
            for part in range(2):
                add_terms(index, columns_of(0, part))

    with jax.named_scope("wait_frame_back"):
        frame_group(frame_res, frame_back, 0, 1, lanes_of_half(1), 7).wait_recv()
        frame_group(frame_res, frame_back, 1, 1, lanes_of_half(1), 14).wait_recv()
    with jax.named_scope("add_terms"):
        for index in range(2):
            for part in range(2):
                add_terms(index, columns_of(1, part))
    put(results.at[1], dq_hbm, 1)
    with jax.named_scope("project"):
        attended = flat(results[0])
        for part in range(4):
            wide = slice(256 * part, 256 * part + 256)
            own_res[0, :, :, wide] = blocks(dot(attended, weight[:, wide], NN).astype(BF16))
        put(own_res.at[0], proj_hbm, 0)

    with jax.named_scope("wait_frame_back"):
        frame_group(frame_res, frame_back, 2, 2, lanes_of_half(1), 11).wait_recv()
    with jax.named_scope("add_terms"):
        for index in range(2, 4):
            for part in range(2):
                add_terms(index, columns_of(1, part))
    put(results.at[2], dk_hbm, 2)
    put(results.at[3], dv_hbm, 3)

    with jax.named_scope("wait_gradient_far"):
        gradient_far().wait_recv()
    total = far_in[0].astype(F32)
    for index in range(1, 8):
        total = total + far_in[index].astype(F32)
    last[...] = (total * (1.0 / 256.0)).astype(BF16)
    put(last, wg_hbm, 4)

    with jax.named_scope("drain"):
        near_weight(0).wait_send()
        near_weight(10).wait_send()
        across.wait_send()
        view_group(own, of_view, 0, 4, 1).wait_send()
        view_group(view_res, view_back, 0, 4, 5).wait_send()
        frame_group(own, of_frame, 3, 1, everything, 2).wait_send()
        for half in range(2):
            frame_group(own, of_frame, 0, 3, lanes_of_half(half), 3 + half).wait_send()
        frame_group(frame_res, frame_back, 0, 1, lanes_of_half(0), 6).wait_send()
        frame_group(frame_res, frame_back, 1, 3, lanes_of_half(0), 13).wait_send()
        frame_group(frame_res, frame_back, 0, 1, lanes_of_half(1), 7).wait_send()
        frame_group(frame_res, frame_back, 1, 1, lanes_of_half(1), 14).wait_send()
        frame_group(frame_res, frame_back, 2, 2, lanes_of_half(1), 11).wait_send()
        gradient_far().wait_send()
        gradient_near().wait_send()
        for copy in slices + passes + to_core + to_chip:
            copy.wait_send()
        for copy in stores:
            copy.wait()


def store(*refs):
    copies = [pltpu.make_async_copy(refs[index], refs[5 + index], refs[10].at[index]) for index in range(5)]
    for copy in copies:
        copy.start()
    for copy in copies:
        copy.wait()


def local(query_rows, key_rows, value_rows, cotangent, out_weight):
    shape = query_rows.shape
    tokens = (16, 8, D)
    rows = [array.reshape(tokens) for array in (query_rows, key_rows, value_rows, cotangent)]
    rows = [pltpu.with_memory_space_constraint(array, pltpu.HBM) for array in rows + [out_weight]]
    four = pltpu.VMEM((4,) + tokens, BF16)
    near = pltpu.VMEM((2, 8, 8, D), BF16)
    probs = pltpu.VMEM((PAIRS, 256, 128), F32)
    dma = pltpu.SemaphoreType.DMA
    out = jax.ShapeDtypeStruct(tokens, BF16)
    outs = pl.pallas_call(
        kernel,
        out_shape=(out, out, out, out, jax.ShapeDtypeStruct((8, D), BF16)),
        in_specs=[pl.BlockSpec(memory_space=pltpu.HBM)] * 5,
        out_specs=(pl.BlockSpec(memory_space=pl.ANY),) * 5,
        scratch_shapes=[
            four, four, four, pltpu.VMEM((64, D), BF16), pltpu.VMEM((D, D), BF16),
            four, four, four, four, four,
            probs, probs, probs, pltpu.VMEM((128, D), BF16), pltpu.VMEM((128, D), BF16), pltpu.VMEM((384, D), BF16),
            four, four, four, four, near, near, pltpu.VMEM((2, 8, D), BF16), pltpu.VMEM((8, 8, D), BF16),
            four, pltpu.VMEM((8, D), BF16),
            dma((5,)), dma((5,)), dma((15,)), dma((15,)), dma((4,)), dma((4,)), dma((4,)), dma((4,)),
            dma((5,)), dma((5,)), dma((5,)), dma((5,)),
        ],
        compiler_params=pltpu.CompilerParams(
            collective_id=0, has_side_effects=True, vmem_limit_bytes=52 * 2**20
        ),
        name="attention",
    )(*rows)
    outs = pl.pallas_call(
        store,
        out_shape=tuple(jax.ShapeDtypeStruct(array.shape, BF16) for array in outs),
        in_specs=[pl.BlockSpec(memory_space=pl.ANY)] * 5,
        out_specs=(pl.BlockSpec(memory_space=pltpu.HBM),) * 5,
        scratch_shapes=[dma((5,))],
        compiler_params=pltpu.CompilerParams(vmem_limit_bytes=2**20),
        name="store",
    )(*outs)
    return tuple(array.reshape(shape) for array in outs[:4]) + (outs[4],)


def solution(mesh):
    tokens = P("dp", "view", "frame", None, None)
    return jax.shard_map(
        local,
        mesh=mesh,
        in_specs=(tokens, tokens, tokens, tokens, P("frame", None)),
        out_specs=(tokens, tokens, tokens, tokens, P(("view", "frame"), None)),
        check_vma=False,
    )
```

```python
import functools

import jax
import jax.numpy as jnp
from jax import lax
from jax.experimental import pallas as pl
from jax.experimental.pallas import tpu as pltpu
from jax.sharding import PartitionSpec as P

F32 = jnp.float32
BF16 = jnp.bfloat16
MESH = pl.DeviceIdType.MESH
NN = (((1,), (0,)), ((), ()))
NT = (((1,), (1,)), ((), ()))
TN = (((0,), (0,)), ((), ()))
MASKED = -1e30

D = 1024
VIEWS = 8
FRAMES = 16
CHIPS = VIEWS // 2
PAIRS = D // 128
HALF = D // 2
SCALE = 0.125


def dot(left, right, dims):
    return lax.dot_general(left, right, dims, preferred_element_type=F32)


def flat(block):
    return block.reshape(block.shape[0] * block.shape[1], block.shape[2])


def blocks(rows):
    return rows.reshape(rows.shape[0] // 8, 8, rows.shape[1])


def lower_lanes():
    return lax.broadcasted_iota(jnp.int32, (128, 128), 1) < 64


def by_head(rows, lower):
    one = lower.astype(F32).astype(BF16)
    other = (1.0 - lower.astype(F32)).astype(BF16)
    return jnp.concatenate([rows * one, rows * other], axis=0)


def group_bias(modulus):
    row = lax.broadcasted_iota(jnp.int32, (128, 128), 0)
    column = lax.broadcasted_iota(jnp.int32, (128, 128), 1)
    same = lax.rem(row, modulus) == lax.rem(column, modulus)
    return jnp.where(same, 0.0, MASKED).astype(F32)


def forward_pair(query, key, value, bias, lower):
    scores = dot(by_head(key, lower), query, NT) * SCALE
    halves = []
    for head in range(2):
        part = scores[128 * head : 128 * head + 128]
        if bias is not None:
            part = part + bias
        raised = jnp.exp(part - jnp.max(part, axis=0, keepdims=True))
        halves.append(raised * (1.0 / jnp.sum(raised, axis=0, keepdims=True)))
    probs = jnp.concatenate(halves, axis=0)
    out = dot(probs.astype(BF16), by_head(value, lower), TN)
    return probs, out


def backward_pair(query, key, value, grad, probs, lower):
    dprob = dot(by_head(value, lower), grad, NT)
    halves = []
    for head in range(2):
        prob = probs[128 * head : 128 * head + 128]
        term = prob * dprob[128 * head : 128 * head + 128]
        halves.append((term - prob * jnp.sum(term, axis=0, keepdims=True)).astype(BF16))
    dscore = jnp.concatenate(halves, axis=0)
    value_grad = dot(probs.astype(BF16), grad, NN)
    value_grad = jnp.where(lower, value_grad[:128], value_grad[128:])
    key_grad = dot(dscore, query, NN)
    key_grad = jnp.where(lower, key_grad[:128], key_grad[128:]) * SCALE
    query_grad = dot(dscore, by_head(key, lower), TN) * SCALE
    return query_grad, key_grad, value_grad


def near_offset(step):
    turn = step - 1
    odd = lax.rem(turn, 2)
    return (turn // 2 + 1) * (1 - 2 * odd)


def frame_offset(step):
    across = lax.rem(step, 2)
    turn = (step - 1) // 2
    odd = lax.rem(turn, 2)
    return across * (4 + ((turn + 1) // 2) * (1 - 2 * odd)) + (1 - across) * near_offset(turn + 1), across


def kernel(
    q_hbm, k_hbm, v_hbm, c_hbm, w_hbm,
    proj_hbm, dq_hbm, dk_hbm, dv_hbm, wg_hbm,
    own, of_view, of_frame, shard, weight,
    own_res, view_res, frame_res, view_back, frame_back,
    own_probs, view_probs, frame_probs, grad, frame_grad, rows,
    core_out, core_in, chip_out, chip_in, near_out, near_in, far_out, far_in,
    results, last,
    load_sem, store_sem, send_sem, recv_sem, core_send, core_recv, chip_send, chip_recv,
    slice_send, slice_recv, pass_send, pass_recv,
):
    sample = lax.axis_index("dp")
    view = lax.axis_index("view")
    frame = lax.axis_index("frame")
    chip = view // 2
    core = lax.rem(view, 2)
    far = frame // 8
    near = lax.rem(frame, 8)
    column = far * 4 + sample
    partner = {"view": chip * 2 + 1 - core}
    opposite = lax.rem(far + 1, 2) * 8 + near
    low = lax.rem(chip, 2)
    halves = (1 - chip // 2, chip // 2)
    others = FRAMES - 1
    way = 1 - 2 * core

    def frame_peer(step):
        by, across = frame_offset(step)
        return lax.rem(far + across, 2) * 8 + lax.rem(near + way * by + 8, 8)

    def near_peer(step):
        return lax.rem(near + way * near_offset(step) + 8, 8)

    def view_peer(step):
        return lax.rem(view + step, VIEWS)

    def column_device(step):
        other = lax.rem(column + step, 8)
        return {"dp": lax.rem(other, 4), "frame": (other // 4) * 8 + near}, other

    def chip_peer(step):
        return lax.rem(chip + step, CHIPS)

    def chip_device(step):
        return {"view": chip_peer(step) * 2 + core}

    def remote(source, target, send, recv, device):
        return pltpu.make_async_remote_copy(
            src_ref=source, dst_ref=target, send_sem=send, recv_sem=recv,
            device_id=device, device_id_type=MESH,
        )

    def group(source, target, slot):
        return remote(source, target, send_sem.at[slot], recv_sem.at[slot], partner)

    def each(first, last_step, body):
        def step(index, carry):
            body(index)
            return carry

        lax.fori_loop(first, last_step, step, 0)

    with jax.named_scope("load_and_greet"):
        loads = [pltpu.make_async_copy(w_hbm, shard, load_sem.at[4])]
        for index, source in enumerate((q_hbm, k_hbm, v_hbm, c_hbm)):
            loads.append(pltpu.make_async_copy(source, own.at[index], load_sem.at[index]))
        for load in loads:
            load.start()
        barrier = pltpu.get_barrier_semaphore()

        def greet(device):
            pl.semaphore_signal(barrier, inc=1, device_id=device, device_id_type=MESH)

        for step in range(1, FRAMES):
            greet({"frame": lax.rem(frame + step, FRAMES)})
        for step in (1, 2, 3, 5, 6, 7):
            greet(column_device(step)[0])
        for step in range(1, VIEWS):
            greet({"view": view_peer(step)})
        pl.semaphore_wait(barrier, FRAMES - 1 + VIEWS - 1 + 6)
        for load in loads:
            load.wait()

    columns = pl.ds(pl.multiple_of(view * 128, 128), 128)

    def shard_rows(which):
        return pl.ds(pl.multiple_of(which * 64, 64), 64)

    across = remote(
        shard.at[:, columns], weight.at[shard_rows(frame), columns], slice_send.at[0], slice_recv.at[0],
        {"frame": opposite},
    )

    def send_weight(source, which, slot):
        def send(step):
            remote(
                source, weight.at[shard_rows(which), columns], send_sem.at[slot], recv_sem.at[slot],
                {"frame": far * 8 + near_peer(step)},
            ).start()

        return send

    def near_weight(slot):
        part = weight.at[pl.ds(0, 64 * 7), columns]
        return group(part, part, slot)

    def send_view(step):
        peer = view_peer(step)
        remote(
            own.at[:, pl.ds(peer * 2, 2)], of_view.at[:, pl.ds(view * 2, 2)], send_sem.at[1], recv_sem.at[1],
            {"view": peer},
        ).start()

    def view_group(source, target, first, count, slot):
        parts, most = pl.ds(first, count), pl.ds(0, 2 * (VIEWS - 1))
        return group(source.at[parts, most], target.at[parts, most], slot)

    def send_frame_grad(step):
        peer = frame_peer(step)
        remote(own.at[3, peer], of_frame.at[3, frame], send_sem.at[2], recv_sem.at[2], {"frame": peer}).start()

    def frame_group(source, target, first, count, lanes, slot):
        parts, most = pl.ds(first, count), pl.ds(0, others)
        return group(source.at[parts, most, :, lanes], target.at[parts, most, :, lanes], slot)

    def lanes_of_half(half):
        return pl.ds(pl.multiple_of(halves[half] * HALF, HALF), HALF)

    def send_frame_rows(half):
        lanes = lanes_of_half(half)

        def send(step):
            peer = frame_peer(step)
            remote(
                own.at[pl.ds(0, 3), peer, :, lanes], of_frame.at[pl.ds(0, 3), frame, :, lanes],
                send_sem.at[3 + half], recv_sem.at[3 + half], {"frame": peer},
            ).start()

        return send

    with jax.named_scope("send_first"):
        across.start()
        each(1, 8, send_weight(shard.at[:, columns], frame, 0))
        each(1, FRAMES, send_frame_grad)
        each(1, VIEWS, send_view)
        weight[shard_rows(frame), columns] = shard[:, columns]
        of_frame[:, pl.ds(frame, 1)] = own[:, pl.ds(frame, 1)]
        of_view[:, pl.ds(view * 2, 2)] = own[:, pl.ds(view * 2, 2)]

    lower = lower_lanes()

    def lanes_of(pair):
        return pl.ds(pl.multiple_of(pair * 128, 128), 128)

    def forward(source, target, kept, bias, first=0, count=PAIRS):
        def step(pair):
            lanes = lanes_of(pair)
            query, key, value = (flat(source[index, :, :, lanes]) for index in range(3))
            probs, out = forward_pair(query, key, value, bias, lower)
            kept[pair] = probs
            target[0, :, :, lanes] = blocks(out.astype(BF16))

        def two(index):
            step(first + index * 2)
            step(first + index * 2 + 1)

        each(0, count // 2, two)

    def grad_rows(source, target, first=0, parts=4):
        cotangent = flat(source[3])
        for part in range(parts):
            wide = pl.ds(pl.multiple_of(first + 256 * part, 256), 256)
            target[:, wide] = dot(cotangent, weight[wide, :], NT).astype(BF16)

    def backward(source, target, kept, grad, first=0, count=PAIRS):
        def step(pair):
            lanes = lanes_of(pair)
            query, key, value = (flat(source[index, :, :, lanes]) for index in range(3))
            grads = backward_pair(query, key, value, grad[:, lanes], kept[pair], lower)
            for index, term in enumerate(grads):
                target[1 + index, :, :, lanes] = blocks(term.astype(BF16))

        def two(index):
            step(first + index * 2)
            step(first + index * 2 + 1)

        each(0, count // 2, two)

    with jax.named_scope("spatial_forward"):
        forward(own, own_res, own_probs, None, 0, PAIRS // 2)
    with jax.named_scope("wait_weight_opposite"):
        across.wait_recv()
    with jax.named_scope("send_weight"):
        each(1, 8, send_weight(weight.at[shard_rows(opposite), columns], opposite, 10))
    with jax.named_scope("spatial_forward"):
        forward(own, own_res, own_probs, None, PAIRS // 2, PAIRS // 2)
    with jax.named_scope("send_frames"):
        each(1, FRAMES, send_frame_rows(0))

    with jax.named_scope("wait_weight_frames"):
        near_weight(0).wait_recv()
        near_weight(10).wait_recv()
    def slice_of(step, first, count):
        came = chip_peer(CHIPS - step) * 2 + core
        return weight.at[pl.ds(first, count), pl.ds(pl.multiple_of(came * 128, 128), 128)]

    def along(step, first, count, index, to):
        part = slice_of(step, first, count)
        copy = remote(part, part, slice_send.at[index], slice_recv.at[index], chip_device(to))
        copy.start()
        return copy

    def to_partner(step, first, count, index):
        part = slice_of(step, first, count)
        copy = remote(part, part, pass_send.at[index], pass_recv.at[index], partner)
        copy.start()
        return copy

    with jax.named_scope("pass_weight"):
        slices = [along(0, 0, D, 1, 1), along(0, 0, D, 3, 3)]
        passes = [to_partner(0, 0, D, 0)]

    with jax.named_scope("wait_view_rows"):
        view_group(own, of_view, 0, 4, 1).wait_recv()
    with jax.named_scope("view_forward"):
        forward(of_view, view_res, view_probs, group_bias(16))
    with jax.named_scope("send_frames"):
        each(1, FRAMES, send_frame_rows(1))

    with jax.named_scope("wait_weight_chips"):
        slices[0].wait_recv()
        slices.append(along(1, 0, HALF, 2, 1))
        slices[1].wait_recv()
        slices.append(along(3, HALF, HALF, 4, 3))
        passes.append(to_partner(1, 0, D, 1))
        passes.append(to_partner(3, 0, D, 3))
    def return_view():
        def send(step):
            peer = view_peer(step)
            remote(
                view_res.at[:, pl.ds(peer * 2, 2)], view_back.at[:, pl.ds(view * 2, 2)],
                send_sem.at[5], recv_sem.at[5], {"view": peer},
            ).start()

        each(1, VIEWS, send)
        view_back[:, pl.ds(view * 2, 2)] = view_res[:, pl.ds(view * 2, 2)]

    def return_frame(half, first, count, slot):
        lanes = lanes_of_half(half)
        parts = pl.ds(first, count)

        def send(step):
            peer = frame_peer(step)
            remote(
                frame_res.at[parts, peer, :, lanes], frame_back.at[parts, frame, :, lanes],
                send_sem.at[slot], recv_sem.at[slot], {"frame": peer},
            ).start()

        each(1, FRAMES, send)
        for index in range(first, first + count):
            frame_back[index, pl.ds(frame, 1), :, lanes] = frame_res[index, pl.ds(frame, 1), :, lanes]

    everything = pl.ds(0, D)
    frame_bias = group_bias(8)

    def frame_forward(half):
        with jax.named_scope("wait_frame_rows"):
            frame_group(own, of_frame, 0, 3, lanes_of_half(half), 3 + half).wait_recv()
        with jax.named_scope("frame_forward"):
            forward(of_frame, frame_res, frame_probs, frame_bias, halves[half] * (PAIRS // 2), PAIRS // 2)

    def frame_backward(half):
        with jax.named_scope("frame_grad"):
            grad_rows(of_frame, frame_grad, halves[half] * HALF, 2)
        with jax.named_scope("frame_backward"):
            backward(of_frame, frame_res, frame_probs, frame_grad, halves[half] * (PAIRS // 2), PAIRS // 2)

    targets = (halves[0] * 2 + low, halves[0] * 2 + 1 - low, halves[1] * 2 + 1 - low, chip)

    def gradient_rows(which):
        lanes = lanes_of(which)
        left = jnp.concatenate(
            [flat(res[0, :, :, lanes]) for res in (own_res, view_res, frame_res)], axis=0
        )
        return [dot(left, rows[:, HALF * part : HALF * part + HALF], TN) for part in range(2)]

    to_core, to_chip = [], []

    def gradient_to_chips(half):
        with jax.named_scope("gradient_to_core"):
            for slot in (2 * half, 2 * half + 1):
                for part, value in enumerate(gradient_rows(targets[slot] * 2 + 1 - core)):
                    core_out[slot, :, :, HALF * part : HALF * part + HALF] = blocks(value.astype(BF16))
                copy = remote(core_out.at[slot], core_in.at[slot], core_send.at[slot], core_recv.at[slot], partner)
                copy.start()
                to_core.append(copy)
        with jax.named_scope("gradient_to_chips"):
            for slot in (2 * half, 2 * half + 1):
                values = gradient_rows(targets[slot] * 2 + core)
                to_core[slot].wait_recv()
                for part, value in enumerate(values):
                    wide = slice(HALF * part, HALF * part + HALF)
                    total = value + flat(core_in[slot, :, :, wide]).astype(F32)
                    chip_out[slot, :, :, wide] = blocks(total.astype(BF16))
                if slot < 3:
                    copy = remote(
                        chip_out.at[slot], chip_in.at[slot], chip_send.at[slot], chip_recv.at[slot],
                        {"view": targets[slot] * 2 + core},
                    )
                    copy.start()
                    to_chip.append(copy)

    with jax.named_scope("wait_weight_chips"):
        slices[2].wait_recv()
        passes.append(to_partner(2, 0, HALF, 2))
        slices[3].wait_recv()
        passes.append(to_partner(2, HALF, HALF, 4))

    frame_forward(0)
    with jax.named_scope("return_frame_out"):
        return_frame(0, 0, 1, 6)
    with jax.named_scope("wait_frame_cotangent"):
        frame_group(own, of_frame, 3, 1, everything, 2).wait_recv()
    with jax.named_scope("wait_weight_core"):
        for onward in passes:
            onward.wait_recv()
    frame_backward(0)
    with jax.named_scope("return_frame"):
        return_frame(0, 1, 3, 13)
    for index, source in enumerate((own, of_view, of_frame)):
        rows[128 * index : 128 * index + 128] = flat(source[3])
    gradient_to_chips(0)

    frame_forward(1)
    with jax.named_scope("return_frame_out"):
        return_frame(1, 0, 1, 7)
    gradient_to_chips(1)
    frame_backward(1)
    with jax.named_scope("return_frame"):
        return_frame(1, 1, 2, 14)

    with jax.named_scope("view_backward"):
        grad_rows(of_view, grad)
        backward(of_view, view_res, view_probs, grad)
    with jax.named_scope("return_view"):
        return_view()

    def gradient_near():
        most = pl.ds(0, 7)
        return group(near_out.at[:, most], near_in.at[:, most], 8)

    def gradient_far():
        part = far_in.at[pl.ds(0, 7)]
        return group(part, part, 9)

    def send_near(step):
        peer = near_peer(step)
        remote(
            near_out.at[:, peer], near_in.at[:, near], send_sem.at[8], recv_sem.at[8], {"frame": far * 8 + peer}
        ).start()

    def send_far(step):
        device, other = column_device(step)
        remote(far_out.at[other // 4], far_in.at[column], send_sem.at[9], recv_sem.at[9], device).start()

    with jax.named_scope("wait_gradient_chips"):
        for copy in to_chip:
            copy.wait_recv()
    with jax.named_scope("gradient_to_near"):
        for part in range(4):
            wide = slice(256 * part, 256 * part + 256)
            total = chip_out[3, :, :, wide].astype(F32)
            for slot in range(3):
                total = total + chip_in[slot, :, :, wide].astype(F32)
            for index in range(2):
                near_out[index, :, :, wide] = total[8 * index : 8 * index + 8].astype(BF16)
        each(1, 8, send_near)
        near_in[:, pl.ds(near, 1)] = near_out[:, pl.ds(near, 1)]

    with jax.named_scope("return_frame"):
        return_frame(1, 3, 1, 11)

    with jax.named_scope("spatial_backward"):
        grad_rows(own, grad)
        backward(own, own_res, own_probs, grad)
    with jax.named_scope("wait_gradient_near"):
        gradient_near().wait_recv()
    with jax.named_scope("gradient_to_far"):
        for index in range(2):
            total = near_in[index, 0].astype(F32)
            for peer in range(1, 8):
                total = total + near_in[index, peer].astype(F32)
            far_out[index] = total.astype(BF16)
        each(1, 8, send_far)
        far_in[pl.ds(column, 1)] = far_out[pl.ds(far, 1)]

    def add_terms(index, lanes):
        total = own_res[index, :, :, lanes].astype(F32) + view_back[index, :, :, lanes].astype(F32)
        total = total + frame_back[index, :, :, lanes].astype(F32)
        results[index, :, :, lanes] = total.astype(BF16)

    stores = []

    def put(source, target, slot):
        stores.append(pltpu.make_async_copy(source, target, store_sem.at[slot]))
        stores[-1].start()

    def columns_of(half, part):
        return pl.ds(pl.multiple_of(halves[half] * HALF + 256 * part, 256), 256)

    with jax.named_scope("wait_view_back"):
        view_group(view_res, view_back, 0, 4, 5).wait_recv()
    with jax.named_scope("wait_frame_back"):
        frame_group(frame_res, frame_back, 0, 1, lanes_of_half(0), 6).wait_recv()
        frame_group(frame_res, frame_back, 1, 3, lanes_of_half(0), 13).wait_recv()
    with jax.named_scope("add_terms"):
        for index in range(4):
            for part in range(2):
                add_terms(index, columns_of(0, part))

    with jax.named_scope("wait_frame_back"):
        frame_group(frame_res, frame_back, 0, 1, lanes_of_half(1), 7).wait_recv()
        frame_group(frame_res, frame_back, 1, 2, lanes_of_half(1), 14).wait_recv()
    with jax.named_scope("add_terms"):
        for index in range(3):
            for part in range(2):
                add_terms(index, columns_of(1, part))
    put(results.at[1], dq_hbm, 1)
    put(results.at[2], dk_hbm, 2)
    with jax.named_scope("project"):
        attended = flat(results[0])
        for part in range(4):
            wide = slice(256 * part, 256 * part + 256)
            own_res[0, :, :, wide] = blocks(dot(attended, weight[:, wide], NN).astype(BF16))
        put(own_res.at[0], proj_hbm, 0)

    with jax.named_scope("wait_frame_back"):
        frame_group(frame_res, frame_back, 3, 1, lanes_of_half(1), 11).wait_recv()
    with jax.named_scope("add_terms"):
        for part in range(2):
            add_terms(3, columns_of(1, part))
    put(results.at[3], dv_hbm, 3)

    with jax.named_scope("wait_gradient_far"):
        gradient_far().wait_recv()
    total = far_in[0].astype(F32)
    for index in range(1, 8):
        total = total + far_in[index].astype(F32)
    last[...] = (total * (1.0 / 256.0)).astype(BF16)
    put(last, wg_hbm, 4)

    with jax.named_scope("drain"):
        near_weight(0).wait_send()
        near_weight(10).wait_send()
        across.wait_send()
        view_group(own, of_view, 0, 4, 1).wait_send()
        view_group(view_res, view_back, 0, 4, 5).wait_send()
        frame_group(own, of_frame, 3, 1, everything, 2).wait_send()
        for half in range(2):
            frame_group(own, of_frame, 0, 3, lanes_of_half(half), 3 + half).wait_send()
        frame_group(frame_res, frame_back, 0, 1, lanes_of_half(0), 6).wait_send()
        frame_group(frame_res, frame_back, 1, 3, lanes_of_half(0), 13).wait_send()
        frame_group(frame_res, frame_back, 0, 1, lanes_of_half(1), 7).wait_send()
        frame_group(frame_res, frame_back, 1, 2, lanes_of_half(1), 14).wait_send()
        frame_group(frame_res, frame_back, 3, 1, lanes_of_half(1), 11).wait_send()
        gradient_far().wait_send()
        gradient_near().wait_send()
        for copy in slices + passes + to_core + to_chip:
            copy.wait_send()
        for copy in stores:
            copy.wait()


def store(*refs):
    copies = [pltpu.make_async_copy(refs[index], refs[5 + index], refs[10].at[index]) for index in range(5)]
    for copy in copies:
        copy.start()
    for copy in copies:
        copy.wait()


def local(query_rows, key_rows, value_rows, cotangent, out_weight):
    shape = query_rows.shape
    tokens = (16, 8, D)
    rows = [array.reshape(tokens) for array in (query_rows, key_rows, value_rows, cotangent)]
    rows = [pltpu.with_memory_space_constraint(array, pltpu.HBM) for array in rows + [out_weight]]
    four = pltpu.VMEM((4,) + tokens, BF16)
    near = pltpu.VMEM((2, 8, 8, D), BF16)
    probs = pltpu.VMEM((PAIRS, 256, 128), F32)
    dma = pltpu.SemaphoreType.DMA
    out = jax.ShapeDtypeStruct(tokens, BF16)
    outs = pl.pallas_call(
        kernel,
        out_shape=(out, out, out, out, jax.ShapeDtypeStruct((8, D), BF16)),
        in_specs=[pl.BlockSpec(memory_space=pltpu.HBM)] * 5,
        out_specs=(pl.BlockSpec(memory_space=pl.ANY),) * 5,
        scratch_shapes=[
            four, four, four, pltpu.VMEM((64, D), BF16), pltpu.VMEM((D, D), BF16),
            four, four, four, four, four,
            probs, probs, probs, pltpu.VMEM((128, D), BF16), pltpu.VMEM((128, D), BF16), pltpu.VMEM((384, D), BF16),
            four, four, four, four, near, near, pltpu.VMEM((2, 8, D), BF16), pltpu.VMEM((8, 8, D), BF16),
            four, pltpu.VMEM((8, D), BF16),
            dma((5,)), dma((5,)), dma((15,)), dma((15,)), dma((4,)), dma((4,)), dma((4,)), dma((4,)),
            dma((5,)), dma((5,)), dma((5,)), dma((5,)),
        ],
        compiler_params=pltpu.CompilerParams(
            collective_id=0, has_side_effects=True, vmem_limit_bytes=52 * 2**20
        ),
        name="attention",
    )(*rows)
    outs = pl.pallas_call(
        store,
        out_shape=tuple(jax.ShapeDtypeStruct(array.shape, BF16) for array in outs),
        in_specs=[pl.BlockSpec(memory_space=pl.ANY)] * 5,
        out_specs=(pl.BlockSpec(memory_space=pltpu.HBM),) * 5,
        scratch_shapes=[dma((5,))],
        compiler_params=pltpu.CompilerParams(vmem_limit_bytes=2**20),
        name="store",
    )(*outs)
    return tuple(array.reshape(shape) for array in outs[:4]) + (outs[4],)


def solution(mesh):
    tokens = P("dp", "view", "frame", None, None)
    return jax.shard_map(
        local,
        mesh=mesh,
        in_specs=(tokens, tokens, tokens, tokens, P("frame", None)),
        out_specs=(tokens, tokens, tokens, tokens, P(("view", "frame"), None)),
        check_vma=False,
    )
```

```python
import functools

import jax
import jax.numpy as jnp
from jax import lax
from jax.experimental import pallas as pl
from jax.experimental.pallas import tpu as pltpu
from jax.sharding import PartitionSpec as P

F32 = jnp.float32
BF16 = jnp.bfloat16
MESH = pl.DeviceIdType.MESH
NN = (((1,), (0,)), ((), ()))
NT = (((1,), (1,)), ((), ()))
TN = (((0,), (0,)), ((), ()))
MASKED = -1e30

D = 1024
VIEWS = 8
FRAMES = 16
CHIPS = VIEWS // 2
PAIRS = D // 128
HALF = D // 2
SCALE = 0.125


def dot(left, right, dims):
    return lax.dot_general(left, right, dims, preferred_element_type=F32)


def flat(block):
    return block.reshape(block.shape[0] * block.shape[1], block.shape[2])


def blocks(rows):
    return rows.reshape(rows.shape[0] // 8, 8, rows.shape[1])


def lower_lanes():
    return lax.broadcasted_iota(jnp.int32, (128, 128), 1) < 64


def by_head(rows, lower):
    one = lower.astype(F32).astype(BF16)
    other = (1.0 - lower.astype(F32)).astype(BF16)
    return jnp.concatenate([rows * one, rows * other], axis=0)


def group_bias(modulus):
    row = lax.broadcasted_iota(jnp.int32, (128, 128), 0)
    column = lax.broadcasted_iota(jnp.int32, (128, 128), 1)
    same = lax.rem(row, modulus) == lax.rem(column, modulus)
    return jnp.where(same, 0.0, MASKED).astype(F32)


def forward_pair(query, key, value, bias, lower):
    scores = dot(by_head(key, lower), query, NT) * SCALE
    halves = []
    for head in range(2):
        part = scores[128 * head : 128 * head + 128]
        if bias is not None:
            part = part + bias
        raised = jnp.exp(part - jnp.max(part, axis=0, keepdims=True))
        halves.append(raised * (1.0 / jnp.sum(raised, axis=0, keepdims=True)))
    probs = jnp.concatenate(halves, axis=0)
    out = dot(probs.astype(BF16), by_head(value, lower), TN)
    return probs, out


def backward_pair(query, key, value, grad, probs, lower):
    dprob = dot(by_head(value, lower), grad, NT)
    halves = []
    for head in range(2):
        prob = probs[128 * head : 128 * head + 128]
        term = prob * dprob[128 * head : 128 * head + 128]
        halves.append((term - prob * jnp.sum(term, axis=0, keepdims=True)).astype(BF16))
    dscore = jnp.concatenate(halves, axis=0)
    value_grad = dot(probs.astype(BF16), grad, NN)
    value_grad = jnp.where(lower, value_grad[:128], value_grad[128:])
    key_grad = dot(dscore, query, NN)
    key_grad = jnp.where(lower, key_grad[:128], key_grad[128:]) * SCALE
    query_grad = dot(dscore, by_head(key, lower), TN) * SCALE
    return query_grad, key_grad, value_grad


def near_offset(step):
    turn = step - 1
    odd = lax.rem(turn, 2)
    return (turn // 2 + 1) * (1 - 2 * odd)


def frame_offset(step):
    across = lax.rem(step, 2)
    turn = (step - 1) // 2
    odd = lax.rem(turn, 2)
    return across * (4 + ((turn + 1) // 2) * (1 - 2 * odd)) + (1 - across) * near_offset(turn + 1), across


def kernel(
    q_hbm, k_hbm, v_hbm, c_hbm, w_hbm,
    proj_hbm, dq_hbm, dk_hbm, dv_hbm, wg_hbm,
    own, of_view, of_frame, shard, weight,
    own_res, view_res, frame_res, view_back, frame_back,
    own_probs, view_probs, frame_probs, grad, frame_grad, rows,
    core_out, core_in, chip_out, chip_in, near_out, near_in, far_out, far_in,
    results, last,
    load_sem, store_sem, send_sem, recv_sem, core_send, core_recv, chip_send, chip_recv,
    slice_send, slice_recv, pass_send, pass_recv,
):
    sample = lax.axis_index("dp")
    view = lax.axis_index("view")
    frame = lax.axis_index("frame")
    chip = view // 2
    core = lax.rem(view, 2)
    far = frame // 8
    near = lax.rem(frame, 8)
    column = far * 4 + sample
    partner = {"view": chip * 2 + 1 - core}
    opposite = lax.rem(far + 1, 2) * 8 + near
    low = lax.rem(chip, 2)
    halves = (1 - chip // 2, chip // 2)
    others = FRAMES - 1
    way = 1 - 2 * core

    def frame_peer(step):
        by, across = frame_offset(step)
        return lax.rem(far + across, 2) * 8 + lax.rem(near + way * by + 8, 8)

    def near_peer(step):
        return lax.rem(near + way * near_offset(step) + 8, 8)

    def view_peer(step):
        return lax.rem(view + step, VIEWS)

    def column_device(step):
        other = lax.rem(column + step, 8)
        return {"dp": lax.rem(other, 4), "frame": (other // 4) * 8 + near}, other

    def chip_peer(step):
        return lax.rem(chip + step, CHIPS)

    def chip_device(step):
        return {"view": chip_peer(step) * 2 + core}

    def remote(source, target, send, recv, device):
        return pltpu.make_async_remote_copy(
            src_ref=source, dst_ref=target, send_sem=send, recv_sem=recv,
            device_id=device, device_id_type=MESH,
        )

    def group(source, target, slot):
        return remote(source, target, send_sem.at[slot], recv_sem.at[slot], partner)

    def each(first, last_step, body):
        def step(index, carry):
            body(index)
            return carry

        lax.fori_loop(first, last_step, step, 0)

    with jax.named_scope("load_and_greet"):
        loads = [pltpu.make_async_copy(w_hbm, shard, load_sem.at[4])]
        for index, source in enumerate((q_hbm, k_hbm, v_hbm, c_hbm)):
            loads.append(pltpu.make_async_copy(source, own.at[index], load_sem.at[index]))
        for load in loads:
            load.start()
        barrier = pltpu.get_barrier_semaphore()

        def greet(device):
            pl.semaphore_signal(barrier, inc=1, device_id=device, device_id_type=MESH)

        for step in range(1, FRAMES):
            greet({"frame": lax.rem(frame + step, FRAMES)})
        for step in (1, 2, 3, 5, 6, 7):
            greet(column_device(step)[0])
        for step in range(1, VIEWS):
            greet({"view": view_peer(step)})
        pl.semaphore_wait(barrier, FRAMES - 1 + VIEWS - 1 + 6)
        for load in loads:
            load.wait()

    columns = pl.ds(pl.multiple_of(view * 128, 128), 128)

    def shard_rows(which):
        return pl.ds(pl.multiple_of(which * 64, 64), 64)

    across = remote(
        shard.at[:, columns], weight.at[shard_rows(frame), columns], slice_send.at[0], slice_recv.at[0],
        {"frame": opposite},
    )

    def send_weight(source, which, slot):
        def send(step):
            remote(
                source, weight.at[shard_rows(which), columns], send_sem.at[slot], recv_sem.at[slot],
                {"frame": far * 8 + near_peer(step)},
            ).start()

        return send

    def near_weight(slot):
        part = weight.at[pl.ds(0, 64 * 7), columns]
        return group(part, part, slot)

    def send_view(step):
        peer = view_peer(step)
        remote(
            own.at[:, pl.ds(peer * 2, 2)], of_view.at[:, pl.ds(view * 2, 2)], send_sem.at[1], recv_sem.at[1],
            {"view": peer},
        ).start()

    def view_group(source, target, first, count, slot):
        parts, most = pl.ds(first, count), pl.ds(0, 2 * (VIEWS - 1))
        return group(source.at[parts, most], target.at[parts, most], slot)

    def send_frame_grad(step):
        peer = frame_peer(step)
        remote(own.at[3, peer], of_frame.at[3, frame], send_sem.at[2], recv_sem.at[2], {"frame": peer}).start()

    def frame_group(source, target, first, count, lanes, slot):
        parts, most = pl.ds(first, count), pl.ds(0, others)
        return group(source.at[parts, most, :, lanes], target.at[parts, most, :, lanes], slot)

    def lanes_of_half(half):
        return pl.ds(pl.multiple_of(halves[half] * HALF, HALF), HALF)

    def send_frame_rows(half):
        lanes = lanes_of_half(half)

        def send(step):
            peer = frame_peer(step)
            remote(
                own.at[pl.ds(0, 3), peer, :, lanes], of_frame.at[pl.ds(0, 3), frame, :, lanes],
                send_sem.at[3 + half], recv_sem.at[3 + half], {"frame": peer},
            ).start()

        return send

    with jax.named_scope("send_first"):
        across.start()
        each(1, 8, send_weight(shard.at[:, columns], frame, 0))
        each(1, FRAMES, send_frame_grad)
        each(1, VIEWS, send_view)
        weight[shard_rows(frame), columns] = shard[:, columns]
        of_frame[:, pl.ds(frame, 1)] = own[:, pl.ds(frame, 1)]
        of_view[:, pl.ds(view * 2, 2)] = own[:, pl.ds(view * 2, 2)]

    lower = lower_lanes()

    def lanes_of(pair):
        return pl.ds(pl.multiple_of(pair * 128, 128), 128)

    def forward(source, target, kept, bias, first=0, count=PAIRS):
        def step(pair):
            lanes = lanes_of(pair)
            query, key, value = (flat(source[index, :, :, lanes]) for index in range(3))
            probs, out = forward_pair(query, key, value, bias, lower)
            kept[pair] = probs
            target[0, :, :, lanes] = blocks(out.astype(BF16))

        def four(index):
            for part in range(4):
                step(first + index * 4 + part)

        each(0, count // 4, four)

    def grad_rows(source, target, first=0, parts=4):
        cotangent = flat(source[3])
        for part in range(parts):
            wide = pl.ds(pl.multiple_of(first + 256 * part, 256), 256)
            target[:, wide] = dot(cotangent, weight[wide, :], NT).astype(BF16)

    def backward(source, target, kept, grad, first=0, count=PAIRS):
        def step(pair):
            lanes = lanes_of(pair)
            query, key, value = (flat(source[index, :, :, lanes]) for index in range(3))
            grads = backward_pair(query, key, value, grad[:, lanes], kept[pair], lower)
            for index, term in enumerate(grads):
                target[1 + index, :, :, lanes] = blocks(term.astype(BF16))

        def four(index):
            for part in range(4):
                step(first + index * 4 + part)

        each(0, count // 4, four)

    with jax.named_scope("spatial_forward"):
        forward(own, own_res, own_probs, None, 0, PAIRS // 2)
    with jax.named_scope("wait_weight_opposite"):
        across.wait_recv()
    with jax.named_scope("send_weight"):
        each(1, 8, send_weight(weight.at[shard_rows(opposite), columns], opposite, 10))
    with jax.named_scope("spatial_forward"):
        forward(own, own_res, own_probs, None, PAIRS // 2, PAIRS // 2)
    with jax.named_scope("send_frames"):
        each(1, FRAMES, send_frame_rows(0))

    with jax.named_scope("wait_weight_frames"):
        near_weight(0).wait_recv()
        near_weight(10).wait_recv()
    def slice_of(step, first, count):
        came = chip_peer(CHIPS - step) * 2 + core
        return weight.at[pl.ds(first, count), pl.ds(pl.multiple_of(came * 128, 128), 128)]

    def along(step, first, count, index, to):
        part = slice_of(step, first, count)
        copy = remote(part, part, slice_send.at[index], slice_recv.at[index], chip_device(to))
        copy.start()
        return copy

    def to_partner(step, first, count, index):
        part = slice_of(step, first, count)
        copy = remote(part, part, pass_send.at[index], pass_recv.at[index], partner)
        copy.start()
        return copy

    with jax.named_scope("pass_weight"):
        slices = [along(0, 0, D, 1, 1), along(0, 0, D, 3, 3)]
        passes = [to_partner(0, 0, D, 0)]

    with jax.named_scope("wait_view_rows"):
        view_group(own, of_view, 0, 4, 1).wait_recv()
    with jax.named_scope("view_forward"):
        forward(of_view, view_res, view_probs, group_bias(16))
    with jax.named_scope("send_frames"):
        each(1, FRAMES, send_frame_rows(1))

    with jax.named_scope("wait_weight_chips"):
        slices[0].wait_recv()
        slices.append(along(1, 0, HALF, 2, 1))
        slices[1].wait_recv()
        slices.append(along(3, HALF, HALF, 4, 3))
        passes.append(to_partner(1, 0, D, 1))
        passes.append(to_partner(3, 0, D, 3))
    def return_view():
        def send(step):
            peer = view_peer(step)
            remote(
                view_res.at[:, pl.ds(peer * 2, 2)], view_back.at[:, pl.ds(view * 2, 2)],
                send_sem.at[5], recv_sem.at[5], {"view": peer},
            ).start()

        each(1, VIEWS, send)
        view_back[:, pl.ds(view * 2, 2)] = view_res[:, pl.ds(view * 2, 2)]

    def return_frame(half, first, count, slot):
        lanes = lanes_of_half(half)
        parts = pl.ds(first, count)

        def send(step):
            peer = frame_peer(step)
            remote(
                frame_res.at[parts, peer, :, lanes], frame_back.at[parts, frame, :, lanes],
                send_sem.at[slot], recv_sem.at[slot], {"frame": peer},
            ).start()

        each(1, FRAMES, send)
        for index in range(first, first + count):
            frame_back[index, pl.ds(frame, 1), :, lanes] = frame_res[index, pl.ds(frame, 1), :, lanes]

    everything = pl.ds(0, D)
    frame_bias = group_bias(8)

    def frame_forward(half):
        with jax.named_scope("wait_frame_rows"):
            frame_group(own, of_frame, 0, 3, lanes_of_half(half), 3 + half).wait_recv()
        with jax.named_scope("frame_forward"):
            forward(of_frame, frame_res, frame_probs, frame_bias, halves[half] * (PAIRS // 2), PAIRS // 2)

    def frame_backward(half):
        with jax.named_scope("frame_grad"):
            grad_rows(of_frame, frame_grad, halves[half] * HALF, 2)
        with jax.named_scope("frame_backward"):
            backward(of_frame, frame_res, frame_probs, frame_grad, halves[half] * (PAIRS // 2), PAIRS // 2)

    targets = (halves[0] * 2 + low, halves[0] * 2 + 1 - low, halves[1] * 2 + 1 - low, chip)

    def gradient_rows(which):
        lanes = lanes_of(which)
        left = jnp.concatenate(
            [flat(res[0, :, :, lanes]) for res in (own_res, view_res, frame_res)], axis=0
        )
        return [dot(left, rows[:, HALF * part : HALF * part + HALF], TN) for part in range(2)]

    to_core, to_chip = [], []

    def gradient_to_chips(half):
        with jax.named_scope("gradient_to_core"):
            for slot in (2 * half, 2 * half + 1):
                for part, value in enumerate(gradient_rows(targets[slot] * 2 + 1 - core)):
                    core_out[slot, :, :, HALF * part : HALF * part + HALF] = blocks(value.astype(BF16))
                copy = remote(core_out.at[slot], core_in.at[slot], core_send.at[slot], core_recv.at[slot], partner)
                copy.start()
                to_core.append(copy)
        with jax.named_scope("gradient_to_chips"):
            for slot in (2 * half, 2 * half + 1):
                values = gradient_rows(targets[slot] * 2 + core)
                to_core[slot].wait_recv()
                for part, value in enumerate(values):
                    wide = slice(HALF * part, HALF * part + HALF)
                    total = value + flat(core_in[slot, :, :, wide]).astype(F32)
                    chip_out[slot, :, :, wide] = blocks(total.astype(BF16))
                if slot < 3:
                    copy = remote(
                        chip_out.at[slot], chip_in.at[slot], chip_send.at[slot], chip_recv.at[slot],
                        {"view": targets[slot] * 2 + core},
                    )
                    copy.start()
                    to_chip.append(copy)

    with jax.named_scope("wait_weight_chips"):
        slices[2].wait_recv()
        passes.append(to_partner(2, 0, HALF, 2))
        slices[3].wait_recv()
        passes.append(to_partner(2, HALF, HALF, 4))

    frame_forward(0)
    with jax.named_scope("return_frame_out"):
        return_frame(0, 0, 1, 6)
    with jax.named_scope("wait_frame_cotangent"):
        frame_group(own, of_frame, 3, 1, everything, 2).wait_recv()
    with jax.named_scope("wait_weight_core"):
        for onward in passes:
            onward.wait_recv()
    frame_backward(0)
    with jax.named_scope("return_frame"):
        return_frame(0, 1, 3, 13)
    for index, source in enumerate((own, of_view, of_frame)):
        rows[128 * index : 128 * index + 128] = flat(source[3])
    gradient_to_chips(0)

    frame_forward(1)
    gradient_to_chips(1)
    frame_backward(1)
    with jax.named_scope("return_frame"):
        return_frame(1, 0, 3, 7)

    with jax.named_scope("view_backward"):
        grad_rows(of_view, grad)
        backward(of_view, view_res, view_probs, grad)
    with jax.named_scope("return_view"):
        return_view()

    def gradient_near():
        most = pl.ds(0, 7)
        return group(near_out.at[:, most], near_in.at[:, most], 8)

    def gradient_far():
        part = far_in.at[pl.ds(0, 7)]
        return group(part, part, 9)

    def send_near(step):
        peer = near_peer(step)
        remote(
            near_out.at[:, peer], near_in.at[:, near], send_sem.at[8], recv_sem.at[8], {"frame": far * 8 + peer}
        ).start()

    def send_far(step):
        device, other = column_device(step)
        remote(far_out.at[other // 4], far_in.at[column], send_sem.at[9], recv_sem.at[9], device).start()

    with jax.named_scope("wait_gradient_chips"):
        for copy in to_chip:
            copy.wait_recv()
    with jax.named_scope("gradient_to_near"):
        for part in range(4):
            wide = slice(256 * part, 256 * part + 256)
            total = chip_out[3, :, :, wide].astype(F32)
            for slot in range(3):
                total = total + chip_in[slot, :, :, wide].astype(F32)
            for index in range(2):
                near_out[index, :, :, wide] = total[8 * index : 8 * index + 8].astype(BF16)
        each(1, 8, send_near)
        near_in[:, pl.ds(near, 1)] = near_out[:, pl.ds(near, 1)]

    with jax.named_scope("spatial_backward"):
        grad_rows(own, grad)
        backward(own, own_res, own_probs, grad)
    with jax.named_scope("return_frame"):
        return_frame(1, 3, 1, 11)

    with jax.named_scope("wait_gradient_near"):
        gradient_near().wait_recv()
    with jax.named_scope("gradient_to_far"):
        for index in range(2):
            total = near_in[index, 0].astype(F32)
            for peer in range(1, 8):
                total = total + near_in[index, peer].astype(F32)
            far_out[index] = total.astype(BF16)
        each(1, 8, send_far)
        far_in[pl.ds(column, 1)] = far_out[pl.ds(far, 1)]

    def add_terms(index, lanes):
        total = own_res[index, :, :, lanes].astype(F32) + view_back[index, :, :, lanes].astype(F32)
        total = total + frame_back[index, :, :, lanes].astype(F32)
        results[index, :, :, lanes] = total.astype(BF16)

    stores = []

    def put(source, target, slot):
        stores.append(pltpu.make_async_copy(source, target, store_sem.at[slot]))
        stores[-1].start()

    def columns_of(half, part):
        return pl.ds(pl.multiple_of(halves[half] * HALF + 256 * part, 256), 256)

    with jax.named_scope("wait_view_back"):
        view_group(view_res, view_back, 0, 4, 5).wait_recv()
    with jax.named_scope("wait_frame_back"):
        frame_group(frame_res, frame_back, 0, 1, lanes_of_half(0), 6).wait_recv()
        frame_group(frame_res, frame_back, 1, 3, lanes_of_half(0), 13).wait_recv()
    with jax.named_scope("add_terms"):
        for index in range(4):
            for part in range(2):
                add_terms(index, columns_of(0, part))

    with jax.named_scope("wait_frame_back"):
        frame_group(frame_res, frame_back, 0, 3, lanes_of_half(1), 7).wait_recv()
    with jax.named_scope("add_terms"):
        for index in range(3):
            for part in range(2):
                add_terms(index, columns_of(1, part))
    put(results.at[1], dq_hbm, 1)
    put(results.at[2], dk_hbm, 2)
    with jax.named_scope("project"):
        attended = flat(results[0])
        for part in range(4):
            wide = slice(256 * part, 256 * part + 256)
            own_res[0, :, :, wide] = blocks(dot(attended, weight[:, wide], NN).astype(BF16))
        put(own_res.at[0], proj_hbm, 0)

    with jax.named_scope("wait_frame_back"):
        frame_group(frame_res, frame_back, 3, 1, lanes_of_half(1), 11).wait_recv()
    with jax.named_scope("add_terms"):
        for part in range(2):
            add_terms(3, columns_of(1, part))
    put(results.at[3], dv_hbm, 3)

    with jax.named_scope("wait_gradient_far"):
        gradient_far().wait_recv()
    total = far_in[0].astype(F32)
    for index in range(1, 8):
        total = total + far_in[index].astype(F32)
    last[...] = (total * (1.0 / 256.0)).astype(BF16)
    put(last, wg_hbm, 4)

    with jax.named_scope("drain"):
        near_weight(0).wait_send()
        near_weight(10).wait_send()
        across.wait_send()
        view_group(own, of_view, 0, 4, 1).wait_send()
        view_group(view_res, view_back, 0, 4, 5).wait_send()
        frame_group(own, of_frame, 3, 1, everything, 2).wait_send()
        for half in range(2):
            frame_group(own, of_frame, 0, 3, lanes_of_half(half), 3 + half).wait_send()
        frame_group(frame_res, frame_back, 0, 1, lanes_of_half(0), 6).wait_send()
        frame_group(frame_res, frame_back, 1, 3, lanes_of_half(0), 13).wait_send()
        frame_group(frame_res, frame_back, 0, 3, lanes_of_half(1), 7).wait_send()
        frame_group(frame_res, frame_back, 3, 1, lanes_of_half(1), 11).wait_send()
        gradient_far().wait_send()
        gradient_near().wait_send()
        for copy in slices + passes + to_core + to_chip:
            copy.wait_send()
        for copy in stores:
            copy.wait()


def store(*refs):
    copies = [pltpu.make_async_copy(refs[index], refs[5 + index], refs[10].at[index]) for index in range(5)]
    for copy in copies:
        copy.start()
    for copy in copies:
        copy.wait()


def local(query_rows, key_rows, value_rows, cotangent, out_weight):
    shape = query_rows.shape
    tokens = (16, 8, D)
    rows = [array.reshape(tokens) for array in (query_rows, key_rows, value_rows, cotangent)]
    rows = [pltpu.with_memory_space_constraint(array, pltpu.HBM) for array in rows + [out_weight]]
    four = pltpu.VMEM((4,) + tokens, BF16)
    near = pltpu.VMEM((2, 8, 8, D), BF16)
    probs = pltpu.VMEM((PAIRS, 256, 128), F32)
    dma = pltpu.SemaphoreType.DMA
    out = jax.ShapeDtypeStruct(tokens, BF16)
    outs = pl.pallas_call(
        kernel,
        out_shape=(out, out, out, out, jax.ShapeDtypeStruct((8, D), BF16)),
        in_specs=[pl.BlockSpec(memory_space=pltpu.HBM)] * 5,
        out_specs=(pl.BlockSpec(memory_space=pl.ANY),) * 5,
        scratch_shapes=[
            four, four, four, pltpu.VMEM((64, D), BF16), pltpu.VMEM((D, D), BF16),
            four, four, four, four, four,
            probs, probs, probs, pltpu.VMEM((128, D), BF16), pltpu.VMEM((128, D), BF16), pltpu.VMEM((384, D), BF16),
            four, four, four, four, near, near, pltpu.VMEM((2, 8, D), BF16), pltpu.VMEM((8, 8, D), BF16),
            four, pltpu.VMEM((8, D), BF16),
            dma((5,)), dma((5,)), dma((15,)), dma((15,)), dma((4,)), dma((4,)), dma((4,)), dma((4,)),
            dma((5,)), dma((5,)), dma((5,)), dma((5,)),
        ],
        compiler_params=pltpu.CompilerParams(
            collective_id=0, has_side_effects=True, vmem_limit_bytes=52 * 2**20
        ),
        name="attention",
    )(*rows)
    outs = pl.pallas_call(
        store,
        out_shape=tuple(jax.ShapeDtypeStruct(array.shape, BF16) for array in outs),
        in_specs=[pl.BlockSpec(memory_space=pl.ANY)] * 5,
        out_specs=(pl.BlockSpec(memory_space=pltpu.HBM),) * 5,
        scratch_shapes=[dma((5,))],
        compiler_params=pltpu.CompilerParams(vmem_limit_bytes=2**20),
        name="store",
    )(*outs)
    return tuple(array.reshape(shape) for array in outs[:4]) + (outs[4],)


def solution(mesh):
    tokens = P("dp", "view", "frame", None, None)
    return jax.shard_map(
        local,
        mesh=mesh,
        in_specs=(tokens, tokens, tokens, tokens, P("frame", None)),
        out_specs=(tokens, tokens, tokens, tokens, P(("view", "frame"), None)),
        check_vma=False,
    )
```

```python
import functools

import jax
import jax.numpy as jnp
from jax import lax
from jax.experimental import pallas as pl
from jax.experimental.pallas import tpu as pltpu
from jax.sharding import PartitionSpec as P

F32 = jnp.float32
BF16 = jnp.bfloat16
MESH = pl.DeviceIdType.MESH
NN = (((1,), (0,)), ((), ()))
NT = (((1,), (1,)), ((), ()))
TN = (((0,), (0,)), ((), ()))
MASKED = -1e30

D = 1024
VIEWS = 8
FRAMES = 16
CHIPS = VIEWS // 2
PAIRS = D // 128
HALF = D // 2
SCALE = 0.125


def dot(left, right, dims):
    return lax.dot_general(left, right, dims, preferred_element_type=F32)


def flat(block):
    return block.reshape(block.shape[0] * block.shape[1], block.shape[2])


def blocks(rows):
    return rows.reshape(rows.shape[0] // 8, 8, rows.shape[1])


def lower_lanes():
    return lax.broadcasted_iota(jnp.int32, (128, 128), 1) < 64


def by_head(rows, lower):
    one = lower.astype(F32).astype(BF16)
    other = (1.0 - lower.astype(F32)).astype(BF16)
    return jnp.concatenate([rows * one, rows * other], axis=0)


def group_bias(modulus):
    row = lax.broadcasted_iota(jnp.int32, (128, 128), 0)
    column = lax.broadcasted_iota(jnp.int32, (128, 128), 1)
    same = lax.rem(row, modulus) == lax.rem(column, modulus)
    return jnp.where(same, 0.0, MASKED).astype(F32)


def forward_pair(query, key, value, bias, lower):
    scores = dot(by_head(key, lower), query, NT) * SCALE
    halves = []
    for head in range(2):
        part = scores[128 * head : 128 * head + 128]
        if bias is not None:
            part = part + bias
        raised = jnp.exp(part - jnp.max(part, axis=0, keepdims=True))
        halves.append(raised * (1.0 / jnp.sum(raised, axis=0, keepdims=True)))
    probs = jnp.concatenate(halves, axis=0)
    out = dot(probs.astype(BF16), by_head(value, lower), TN)
    return probs, out


def backward_pair(query, key, value, grad, probs, lower):
    dprob = dot(by_head(value, lower), grad, NT)
    halves = []
    for head in range(2):
        prob = probs[128 * head : 128 * head + 128]
        term = prob * dprob[128 * head : 128 * head + 128]
        halves.append((term - prob * jnp.sum(term, axis=0, keepdims=True)).astype(BF16))
    dscore = jnp.concatenate(halves, axis=0)
    value_grad = dot(probs.astype(BF16), grad, NN)
    value_grad = jnp.where(lower, value_grad[:128], value_grad[128:])
    key_grad = dot(dscore, query, NN)
    key_grad = jnp.where(lower, key_grad[:128], key_grad[128:]) * SCALE
    query_grad = dot(dscore, by_head(key, lower), TN) * SCALE
    return query_grad, key_grad, value_grad


def near_offset(step):
    turn = step - 1
    odd = lax.rem(turn, 2)
    return (turn // 2 + 1) * (1 - 2 * odd)


def frame_offset(step):
    across = lax.rem(step, 2)
    turn = (step - 1) // 2
    odd = lax.rem(turn, 2)
    return across * (4 + ((turn + 1) // 2) * (1 - 2 * odd)) + (1 - across) * near_offset(turn + 1), across


def kernel(
    q_hbm, k_hbm, v_hbm, c_hbm, w_hbm,
    proj_hbm, dq_hbm, dk_hbm, dv_hbm, wg_hbm,
    own, of_view, of_frame, shard, weight,
    own_res, view_res, frame_res, view_back, frame_back,
    own_probs, view_probs, frame_probs, grad, frame_grad, rows,
    core_out, core_in, chip_out, chip_in, near_out, near_in, far_out, far_in,
    results, last,
    load_sem, store_sem, send_sem, recv_sem, core_send, core_recv, chip_send, chip_recv,
    slice_send, slice_recv, pass_send, pass_recv,
):
    sample = lax.axis_index("dp")
    view = lax.axis_index("view")
    frame = lax.axis_index("frame")
    chip = view // 2
    core = lax.rem(view, 2)
    far = frame // 8
    near = lax.rem(frame, 8)
    column = far * 4 + sample
    partner = {"view": chip * 2 + 1 - core}
    opposite = lax.rem(far + 1, 2) * 8 + near
    low = lax.rem(chip, 2)
    halves = (1 - chip // 2, chip // 2)
    others = FRAMES - 1
    way = 1 - 2 * core

    def frame_peer(step):
        by, across = frame_offset(step)
        return lax.rem(far + across, 2) * 8 + lax.rem(near + way * by + 8, 8)

    def near_peer(step):
        return lax.rem(near + way * near_offset(step) + 8, 8)

    def view_peer(step):
        return lax.rem(view + step, VIEWS)

    def column_device(step):
        other = lax.rem(column + step, 8)
        return {"dp": lax.rem(other, 4), "frame": (other // 4) * 8 + near}, other

    def chip_peer(step):
        return lax.rem(chip + step, CHIPS)

    def chip_device(step):
        return {"view": chip_peer(step) * 2 + core}

    def remote(source, target, send, recv, device):
        return pltpu.make_async_remote_copy(
            src_ref=source, dst_ref=target, send_sem=send, recv_sem=recv,
            device_id=device, device_id_type=MESH,
        )

    def group(source, target, slot):
        return remote(source, target, send_sem.at[slot], recv_sem.at[slot], partner)

    def each(first, last_step, body):
        def step(index, carry):
            body(index)
            return carry

        lax.fori_loop(first, last_step, step, 0)

    with jax.named_scope("load_and_greet"):
        loads = [pltpu.make_async_copy(w_hbm, shard, load_sem.at[4])]
        for index, source in enumerate((q_hbm, k_hbm, v_hbm, c_hbm)):
            loads.append(pltpu.make_async_copy(source, own.at[index], load_sem.at[index]))
        for load in loads:
            load.start()
        barrier = pltpu.get_barrier_semaphore()

        def greet(device):
            pl.semaphore_signal(barrier, inc=1, device_id=device, device_id_type=MESH)

        for step in range(1, FRAMES):
            greet({"frame": lax.rem(frame + step, FRAMES)})
        for step in (1, 2, 3, 5, 6, 7):
            greet(column_device(step)[0])
        for step in range(1, VIEWS):
            greet({"view": view_peer(step)})
        pl.semaphore_wait(barrier, FRAMES - 1 + VIEWS - 1 + 6)
        loads[0].wait()

    columns = pl.ds(pl.multiple_of(view * 128, 128), 128)

    def shard_rows(which):
        return pl.ds(pl.multiple_of(which * 64, 64), 64)

    across = remote(
        shard.at[:, columns], weight.at[shard_rows(frame), columns], slice_send.at[0], slice_recv.at[0],
        {"frame": opposite},
    )

    def send_weight(source, which, slot):
        def send(step):
            remote(
                source, weight.at[shard_rows(which), columns], send_sem.at[slot], recv_sem.at[slot],
                {"frame": far * 8 + near_peer(step)},
            ).start()

        return send

    def near_weight(slot):
        part = weight.at[pl.ds(0, 64 * 7), columns]
        return group(part, part, slot)

    def send_view(step):
        peer = view_peer(step)
        remote(
            own.at[:, pl.ds(peer * 2, 2)], of_view.at[:, pl.ds(view * 2, 2)], send_sem.at[1], recv_sem.at[1],
            {"view": peer},
        ).start()

    def view_group(source, target, first, count, slot):
        parts, most = pl.ds(first, count), pl.ds(0, 2 * (VIEWS - 1))
        return group(source.at[parts, most], target.at[parts, most], slot)

    def send_frame_grad(step):
        peer = frame_peer(step)
        remote(own.at[3, peer], of_frame.at[3, frame], send_sem.at[2], recv_sem.at[2], {"frame": peer}).start()

    def frame_group(source, target, first, count, lanes, slot):
        parts, most = pl.ds(first, count), pl.ds(0, others)
        return group(source.at[parts, most, :, lanes], target.at[parts, most, :, lanes], slot)

    def lanes_of_half(half):
        return pl.ds(pl.multiple_of(halves[half] * HALF, HALF), HALF)

    def send_frame_rows(half):
        lanes = lanes_of_half(half)

        def send(step):
            peer = frame_peer(step)
            remote(
                own.at[pl.ds(0, 3), peer, :, lanes], of_frame.at[pl.ds(0, 3), frame, :, lanes],
                send_sem.at[3 + half], recv_sem.at[3 + half], {"frame": peer},
            ).start()

        return send

    with jax.named_scope("send_first"):
        across.start()
        each(1, 8, send_weight(shard.at[:, columns], frame, 0))
        for load in loads[1:]:
            load.wait()
        each(1, FRAMES, send_frame_grad)
        each(1, VIEWS, send_view)
        weight[shard_rows(frame), columns] = shard[:, columns]
        of_frame[:, pl.ds(frame, 1)] = own[:, pl.ds(frame, 1)]
        of_view[:, pl.ds(view * 2, 2)] = own[:, pl.ds(view * 2, 2)]

    lower = lower_lanes()

    def lanes_of(pair):
        return pl.ds(pl.multiple_of(pair * 128, 128), 128)

    def forward(source, target, kept, bias, first=0, count=PAIRS):
        def step(pair):
            lanes = lanes_of(pair)
            query, key, value = (flat(source[index, :, :, lanes]) for index in range(3))
            probs, out = forward_pair(query, key, value, bias, lower)
            kept[pair] = probs
            target[0, :, :, lanes] = blocks(out.astype(BF16))

        def four(index):
            for part in range(4):
                step(first + index * 4 + part)

        each(0, count // 4, four)

    def grad_rows(source, target, first=0, parts=4):
        cotangent = flat(source[3])
        for part in range(parts):
            wide = pl.ds(pl.multiple_of(first + 256 * part, 256), 256)
            target[:, wide] = dot(cotangent, weight[wide, :], NT).astype(BF16)

    def backward(source, target, kept, grad, first=0, count=PAIRS):
        def step(pair):
            lanes = lanes_of(pair)
            query, key, value = (flat(source[index, :, :, lanes]) for index in range(3))
            grads = backward_pair(query, key, value, grad[:, lanes], kept[pair], lower)
            for index, term in enumerate(grads):
                target[1 + index, :, :, lanes] = blocks(term.astype(BF16))

        def four(index):
            for part in range(4):
                step(first + index * 4 + part)

        each(0, count // 4, four)

    with jax.named_scope("spatial_forward"):
        forward(own, own_res, own_probs, None, 0, PAIRS // 2)
    with jax.named_scope("wait_weight_opposite"):
        across.wait_recv()
    with jax.named_scope("send_weight"):
        each(1, 8, send_weight(weight.at[shard_rows(opposite), columns], opposite, 10))
    with jax.named_scope("spatial_forward"):
        forward(own, own_res, own_probs, None, PAIRS // 2, PAIRS // 2)
    with jax.named_scope("send_frames"):
        each(1, FRAMES, send_frame_rows(0))

    with jax.named_scope("wait_weight_frames"):
        near_weight(0).wait_recv()
        near_weight(10).wait_recv()
    def slice_of(step, first, count):
        came = chip_peer(CHIPS - step) * 2 + core
        return weight.at[pl.ds(first, count), pl.ds(pl.multiple_of(came * 128, 128), 128)]

    def along(step, first, count, index, to):
        part = slice_of(step, first, count)
        copy = remote(part, part, slice_send.at[index], slice_recv.at[index], chip_device(to))
        copy.start()
        return copy

    def to_partner(step, first, count, index):
        part = slice_of(step, first, count)
        copy = remote(part, part, pass_send.at[index], pass_recv.at[index], partner)
        copy.start()
        return copy

    with jax.named_scope("pass_weight"):
        slices = [along(0, 0, D, 1, 1), along(0, 0, D, 3, 3)]
        passes = [to_partner(0, 0, D, 0)]

    with jax.named_scope("wait_view_rows"):
        view_group(own, of_view, 0, 4, 1).wait_recv()
    with jax.named_scope("view_forward"):
        forward(of_view, view_res, view_probs, group_bias(16))
    with jax.named_scope("send_frames"):
        each(1, FRAMES, send_frame_rows(1))

    with jax.named_scope("wait_weight_chips"):
        slices[0].wait_recv()
        slices.append(along(1, 0, HALF, 2, 1))
        slices[1].wait_recv()
        slices.append(along(3, HALF, HALF, 4, 3))
        passes.append(to_partner(1, 0, D, 1))
        passes.append(to_partner(3, 0, D, 3))
    def return_view():
        def send(step):
            peer = view_peer(step)
            remote(
                view_res.at[:, pl.ds(peer * 2, 2)], view_back.at[:, pl.ds(view * 2, 2)],
                send_sem.at[5], recv_sem.at[5], {"view": peer},
            ).start()

        each(1, VIEWS, send)
        view_back[:, pl.ds(view * 2, 2)] = view_res[:, pl.ds(view * 2, 2)]

    def return_frame(half, first, count, slot):
        lanes = lanes_of_half(half)
        parts = pl.ds(first, count)

        def send(step):
            peer = frame_peer(step)
            remote(
                frame_res.at[parts, peer, :, lanes], frame_back.at[parts, frame, :, lanes],
                send_sem.at[slot], recv_sem.at[slot], {"frame": peer},
            ).start()

        each(1, FRAMES, send)
        for index in range(first, first + count):
            frame_back[index, pl.ds(frame, 1), :, lanes] = frame_res[index, pl.ds(frame, 1), :, lanes]

    everything = pl.ds(0, D)
    frame_bias = group_bias(8)

    def frame_forward(half):
        with jax.named_scope("wait_frame_rows"):
            frame_group(own, of_frame, 0, 3, lanes_of_half(half), 3 + half).wait_recv()
        with jax.named_scope("frame_forward"):
            forward(of_frame, frame_res, frame_probs, frame_bias, halves[half] * (PAIRS // 2), PAIRS // 2)

    def frame_backward(half):
        with jax.named_scope("frame_backward"):
            backward(of_frame, frame_res, frame_probs, frame_grad, halves[half] * (PAIRS // 2), PAIRS // 2)

    targets = (halves[0] * 2 + low, halves[0] * 2 + 1 - low, halves[1] * 2 + 1 - low, chip)

    def gradient_rows(which):
        lanes = lanes_of(which)
        left = jnp.concatenate(
            [flat(res[0, :, :, lanes]) for res in (own_res, view_res, frame_res)], axis=0
        )
        return [dot(left, rows[:, HALF * part : HALF * part + HALF], TN) for part in range(2)]

    to_core, to_chip = [], []

    def gradient_to_chips(half):
        with jax.named_scope("gradient_to_core"):
            for slot in (2 * half, 2 * half + 1):
                for part, value in enumerate(gradient_rows(targets[slot] * 2 + 1 - core)):
                    core_out[slot, :, :, HALF * part : HALF * part + HALF] = blocks(value.astype(BF16))
                copy = remote(core_out.at[slot], core_in.at[slot], core_send.at[slot], core_recv.at[slot], partner)
                copy.start()
                to_core.append(copy)
        with jax.named_scope("gradient_to_chips"):
            for slot in (2 * half, 2 * half + 1):
                values = gradient_rows(targets[slot] * 2 + core)
                to_core[slot].wait_recv()
                for part, value in enumerate(values):
                    wide = slice(HALF * part, HALF * part + HALF)
                    total = value + flat(core_in[slot, :, :, wide]).astype(F32)
                    chip_out[slot, :, :, wide] = blocks(total.astype(BF16))
                if slot < 3:
                    copy = remote(
                        chip_out.at[slot], chip_in.at[slot], chip_send.at[slot], chip_recv.at[slot],
                        {"view": targets[slot] * 2 + core},
                    )
                    copy.start()
                    to_chip.append(copy)

    with jax.named_scope("wait_weight_chips"):
        slices[2].wait_recv()
        passes.append(to_partner(2, 0, HALF, 2))
        slices[3].wait_recv()
        passes.append(to_partner(2, HALF, HALF, 4))

    frame_forward(0)
    with jax.named_scope("return_frame_out"):
        return_frame(0, 0, 1, 6)
    with jax.named_scope("wait_frame_cotangent"):
        frame_group(own, of_frame, 3, 1, everything, 2).wait_recv()
    with jax.named_scope("wait_weight_core"):
        for onward in passes:
            onward.wait_recv()
    def frame_grads(half):
        with jax.named_scope("frame_grad"):
            grad_rows(of_frame, frame_grad, halves[half] * HALF, 2)

    frame_grads(0)
    frame_backward(0)
    with jax.named_scope("return_frame"):
        return_frame(0, 1, 3, 13)
    for index, source in enumerate((own, of_view, of_frame)):
        rows[128 * index : 128 * index + 128] = flat(source[3])
    gradient_to_chips(0)

    frame_grads(1)
    frame_forward(1)
    gradient_to_chips(1)
    frame_backward(1)
    with jax.named_scope("return_frame"):
        return_frame(1, 0, 3, 7)

    with jax.named_scope("view_backward"):
        grad_rows(of_view, grad)
        backward(of_view, view_res, view_probs, grad)
    with jax.named_scope("return_view"):
        return_view()

    def gradient_near():
        most = pl.ds(0, 7)
        return group(near_out.at[:, most], near_in.at[:, most], 8)

    def gradient_far():
        part = far_in.at[pl.ds(0, 7)]
        return group(part, part, 9)

    def send_near(step):
        peer = near_peer(step)
        remote(
            near_out.at[:, peer], near_in.at[:, near], send_sem.at[8], recv_sem.at[8], {"frame": far * 8 + peer}
        ).start()

    def send_far(step):
        device, other = column_device(step)
        remote(far_out.at[other // 4], far_in.at[column], send_sem.at[9], recv_sem.at[9], device).start()

    with jax.named_scope("wait_gradient_chips"):
        for copy in to_chip:
            copy.wait_recv()
    with jax.named_scope("gradient_to_near"):
        for part in range(4):
            wide = slice(256 * part, 256 * part + 256)
            total = chip_out[3, :, :, wide].astype(F32)
            for slot in range(3):
                total = total + chip_in[slot, :, :, wide].astype(F32)
            for index in range(2):
                near_out[index, :, :, wide] = total[8 * index : 8 * index + 8].astype(BF16)
        each(1, 8, send_near)
        near_in[:, pl.ds(near, 1)] = near_out[:, pl.ds(near, 1)]

    with jax.named_scope("spatial_backward"):
        grad_rows(own, grad)
        backward(own, own_res, own_probs, grad)
    with jax.named_scope("return_frame"):
        return_frame(1, 3, 1, 11)

    with jax.named_scope("wait_gradient_near"):
        gradient_near().wait_recv()
    with jax.named_scope("gradient_to_far"):
        for index in range(2):
            total = near_in[index, 0].astype(F32)
            for peer in range(1, 8):
                total = total + near_in[index, peer].astype(F32)
            far_out[index] = total.astype(BF16)
        each(1, 8, send_far)
        far_in[pl.ds(column, 1)] = far_out[pl.ds(far, 1)]

    def add_terms(index, lanes):
        total = own_res[index, :, :, lanes].astype(F32) + view_back[index, :, :, lanes].astype(F32)
        total = total + frame_back[index, :, :, lanes].astype(F32)
        results[index, :, :, lanes] = total.astype(BF16)

    stores = []

    def put(source, target, slot):
        stores.append(pltpu.make_async_copy(source, target, store_sem.at[slot]))
        stores[-1].start()

    def columns_of(half, part):
        return pl.ds(pl.multiple_of(halves[half] * HALF + 256 * part, 256), 256)

    with jax.named_scope("wait_view_back"):
        view_group(view_res, view_back, 0, 4, 5).wait_recv()
    with jax.named_scope("wait_frame_back"):
        frame_group(frame_res, frame_back, 0, 1, lanes_of_half(0), 6).wait_recv()
        frame_group(frame_res, frame_back, 1, 3, lanes_of_half(0), 13).wait_recv()
    with jax.named_scope("add_terms"):
        for index in range(4):
            for part in range(2):
                add_terms(index, columns_of(0, part))

    with jax.named_scope("wait_frame_back"):
        frame_group(frame_res, frame_back, 0, 3, lanes_of_half(1), 7).wait_recv()
    with jax.named_scope("add_terms"):
        for index in range(3):
            for part in range(2):
                add_terms(index, columns_of(1, part))
    put(results.at[1], dq_hbm, 1)
    put(results.at[2], dk_hbm, 2)
    with jax.named_scope("project"):
        attended = flat(results[0])
        for part in range(4):
            wide = slice(256 * part, 256 * part + 256)
            own_res[0, :, :, wide] = blocks(dot(attended, weight[:, wide], NN).astype(BF16))
        put(own_res.at[0], proj_hbm, 0)

    with jax.named_scope("wait_frame_back"):
        frame_group(frame_res, frame_back, 3, 1, lanes_of_half(1), 11).wait_recv()
    with jax.named_scope("add_terms"):
        for part in range(2):
            add_terms(3, columns_of(1, part))
    put(results.at[3], dv_hbm, 3)

    with jax.named_scope("wait_gradient_far"):
        gradient_far().wait_recv()
    total = far_in[0].astype(F32)
    for index in range(1, 8):
        total = total + far_in[index].astype(F32)
    last[...] = (total * (1.0 / 256.0)).astype(BF16)
    put(last, wg_hbm, 4)

    with jax.named_scope("drain"):
        near_weight(0).wait_send()
        near_weight(10).wait_send()
        across.wait_send()
        view_group(own, of_view, 0, 4, 1).wait_send()
        view_group(view_res, view_back, 0, 4, 5).wait_send()
        frame_group(own, of_frame, 3, 1, everything, 2).wait_send()
        for half in range(2):
            frame_group(own, of_frame, 0, 3, lanes_of_half(half), 3 + half).wait_send()
        frame_group(frame_res, frame_back, 0, 1, lanes_of_half(0), 6).wait_send()
        frame_group(frame_res, frame_back, 1, 3, lanes_of_half(0), 13).wait_send()
        frame_group(frame_res, frame_back, 0, 3, lanes_of_half(1), 7).wait_send()
        frame_group(frame_res, frame_back, 3, 1, lanes_of_half(1), 11).wait_send()
        gradient_far().wait_send()
        gradient_near().wait_send()
        for copy in slices + passes + to_core + to_chip:
            copy.wait_send()
        for copy in stores:
            copy.wait()


def store(*refs):
    copies = [pltpu.make_async_copy(refs[index], refs[5 + index], refs[10].at[index]) for index in range(5)]
    for copy in copies:
        copy.start()
    for copy in copies:
        copy.wait()


def local(query_rows, key_rows, value_rows, cotangent, out_weight):
    shape = query_rows.shape
    tokens = (16, 8, D)
    rows = [array.reshape(tokens) for array in (query_rows, key_rows, value_rows, cotangent)]
    rows = [pltpu.with_memory_space_constraint(array, pltpu.HBM) for array in rows + [out_weight]]
    four = pltpu.VMEM((4,) + tokens, BF16)
    near = pltpu.VMEM((2, 8, 8, D), BF16)
    probs = pltpu.VMEM((PAIRS, 256, 128), F32)
    dma = pltpu.SemaphoreType.DMA
    out = jax.ShapeDtypeStruct(tokens, BF16)
    outs = pl.pallas_call(
        kernel,
        out_shape=(out, out, out, out, jax.ShapeDtypeStruct((8, D), BF16)),
        in_specs=[pl.BlockSpec(memory_space=pltpu.HBM)] * 5,
        out_specs=(pl.BlockSpec(memory_space=pl.ANY),) * 5,
        scratch_shapes=[
            four, four, four, pltpu.VMEM((64, D), BF16), pltpu.VMEM((D, D), BF16),
            four, four, four, four, four,
            probs, probs, probs, pltpu.VMEM((128, D), BF16), pltpu.VMEM((128, D), BF16), pltpu.VMEM((384, D), BF16),
            four, four, four, four, near, near, pltpu.VMEM((2, 8, D), BF16), pltpu.VMEM((8, 8, D), BF16),
            four, pltpu.VMEM((8, D), BF16),
            dma((5,)), dma((5,)), dma((15,)), dma((15,)), dma((4,)), dma((4,)), dma((4,)), dma((4,)),
            dma((5,)), dma((5,)), dma((5,)), dma((5,)),
        ],
        compiler_params=pltpu.CompilerParams(
            collective_id=0, has_side_effects=True, vmem_limit_bytes=52 * 2**20
        ),
        name="attention",
    )(*rows)
    outs = pl.pallas_call(
        store,
        out_shape=tuple(jax.ShapeDtypeStruct(array.shape, BF16) for array in outs),
        in_specs=[pl.BlockSpec(memory_space=pl.ANY)] * 5,
        out_specs=(pl.BlockSpec(memory_space=pltpu.HBM),) * 5,
        scratch_shapes=[dma((5,))],
        compiler_params=pltpu.CompilerParams(vmem_limit_bytes=2**20),
        name="store",
    )(*outs)
    return tuple(array.reshape(shape) for array in outs[:4]) + (outs[4],)


def solution(mesh):
    tokens = P("dp", "view", "frame", None, None)
    return jax.shard_map(
        local,
        mesh=mesh,
        in_specs=(tokens, tokens, tokens, tokens, P("frame", None)),
        out_specs=(tokens, tokens, tokens, tokens, P(("view", "frame"), None)),
        check_vma=False,
    )
```
